32 devices in a mesh: gz: 8 (over z, y), gy: 4 (over x, core).
Axes of the slice: x: 2, y: 2, z: 4, core: 2. Of those that a mesh axis runs over, the one named last changes fastest.
Arguments:
- test_vectors: float32 [4, 32, 384, 256], P(None, 'gz', 'gy'), may hold values from -18 to 18
- conductivity: float32 [32, 384, 256], P('gz', 'gy'), may hold values from 0.1 to 10
Outputs:
- prolongator: float32 [4, 32, 384, 256], P(None, 'gz', 'gy')
- coarse_factors: float32 [10, 8, 96, 64], P(None, 'gz', 'gy')
The draws below stay inside these ranges and needn't reach their ends.
All inputs are finite; a program needn't handle non-finite values.
Results may differ from the reference program's by a relative error of at most 0.0003.
Values sent between devices are 32-bit elements; how exact they have to be, the bound alone decides.
No kernel may reach another device: no remote copies, remote signals or barrier semaphores. Data moves between devices by JAX's collectives and lax.ppermute only.
A program may use at most 64 MiB of HBM per device.

```python
import math
import jax
import jax.numpy as jnp
from jax import lax

CZ = 4
CY = 96
NX = 256
NZ = 32
NY = 384


def draw_test_vectors(key, part):
    first_key = jax.random.fold_in(jax.random.fold_in(key, 11), 0)
    third_key = jax.random.fold_in(jax.random.fold_in(key, 11), 2)
    fourth_key = jax.random.fold_in(jax.random.fold_in(key, 11), 3)
    envelope_key = jax.random.fold_in(key, 29)
    z_ramp = 1.0 + 2.0 * jnp.arange(NZ, dtype=jnp.float32) / NZ
    z_ramp = z_ramp[None, :, None, None]
    ordering = jax.random.permutation(third_key, 4)
    levels = jnp.array([0.1, 0.3, 0.6, 1.0], jnp.float32)
    amplitude = levels[ordering] * jax.random.uniform(fourth_key, (4,), jnp.float32, 0.8, 1.0)
    amplitude = amplitude[:, None, None, None]
    log_env = jax.random.uniform(envelope_key, (4, NZ // CZ, NY // CY), jnp.float32, -2.302585, 0.0)
    envelope = jnp.exp(log_env)
    envelope = jnp.repeat(jnp.repeat(envelope, CZ, axis=1), CY, axis=2)[:, :, :, None]
    values = jnp.clip(jax.random.normal(first_key, (4, NZ, NY, NX), jnp.float32), -6.0, 6.0) * z_ramp * amplitude * envelope
    return values.astype(jnp.float32)


def shard_levels(own_key, shape, cuts, low, largest):
    factor_of = 1.0
    for axis_at, shards_of in cuts:
        draws = jax.random.uniform(jax.random.fold_in(jax.random.fold_in(own_key, 6), axis_at), (shards_of,), jnp.float32, low / len(cuts), largest / len(cuts))
        factor_of = factor_of * jnp.repeat(jnp.exp(draws), shape[axis_at] // shards_of).reshape((-1,) + (1,) * (len(shape) - 1 - axis_at))
    return factor_of


def setup_inputs(seed: int = 0) -> dict:
    arg_keys = jax.random.split(jax.random.key(seed), 3)
    test_vectors = draw_test_vectors(jax.random.fold_in(arg_keys[2], 71), 0)
    conductivity = jnp.clip(jnp.exp(math.log(10.0) - 4.6051702 * jax.random.uniform(arg_keys[1], (NZ, NY, NX), jnp.float32) ** shard_levels(arg_keys[1], (NZ, NY, NX), ((0, 8), (1, 4)), -0.2, 0.2)), 0.1, 10.0)
    return dict(test_vectors=test_vectors, conductivity=conductivity)


RELAX_WEIGHT = 2.0 / 3.0
PAIR_LIST = ((0, 0), (0, 1), (0, 2), (0, 3), (1, 1), (1, 2), (1, 3), (2, 2), (2, 3), (3, 3))

def sweep(values_ext, coef_ext):
    center_coef = coef_ext[1:-1, 1:-1]
    center_vals = values_ext[:, 1:-1, 1:-1]
    neighbours = [(coef_ext[2:, 1:-1], values_ext[:, 2:, 1:-1]), (coef_ext[:-2, 1:-1], values_ext[:, :-2, 1:-1]), (coef_ext[1:-1, 2:], values_ext[:, 1:-1, 2:]), (coef_ext[1:-1, :-2], values_ext[:, 1:-1, :-2]), (jnp.roll(center_coef, -1, axis=-1), jnp.roll(center_vals, -1, axis=-1)), (jnp.roll(center_coef, 1, axis=-1), jnp.roll(center_vals, 1, axis=-1))]
    diagonal = jnp.zeros_like(center_coef)
    fluxes = jnp.zeros_like(center_vals)
    for next_coef, next_vals in neighbours:
        weight = 2.0 * center_coef * next_coef / (center_coef + next_coef)
        diagonal = diagonal + weight
        fluxes = fluxes + weight * (center_vals - next_vals)
    return center_vals - RELAX_WEIGHT * fluxes / diagonal

def block_table(across):
    cells = jnp.arange(across) // 4
    return (cells[:, None] == jnp.arange(across // 4)[None, :]).astype(jnp.float32)

def pair_products(fields):
    return jnp.stack([fields[left_idx] * fields[right_idx] for left_idx, right_idx in PAIR_LIST])

def block_sums(values):
    number, layers, height, across = values.shape
    folded = values.reshape(number, layers // 4, 4, height // 4, 4, across).sum(axis=(2, 4))
    flat = jnp.dot(folded.reshape(-1, across), block_table(across), precision=lax.Precision.HIGHEST)
    return flat.reshape(number, layers // 4, height // 4, across // 4)

def spread_blocks(values, across):
    number, layers, height, blocks_x = values.shape
    flat = jnp.dot(values.reshape(-1, blocks_x), block_table(across).T, precision=lax.Precision.HIGHEST)
    spread = flat.reshape(number, layers, height, across)
    spread = jnp.repeat(spread, 4, axis=1)
    return jnp.repeat(spread, 4, axis=2)

def factor(blocks, grams):
    matrix = [[None] * 4 for _ in range(4)]
    for position, pair in enumerate(PAIR_LIST):
        matrix[pair[0]][pair[1]] = grams[position]
    trace = matrix[0][0] + matrix[1][1] + matrix[2][2] + matrix[3][3]
    ridge = 0.64 * (trace / 256.0 + 1e-06)
    upper = [[None] * 4 for _ in range(4)]
    for row_index in range(4):
        for col_index in range(row_index, 4):
            accum = matrix[row_index][col_index]
            if row_index == col_index:
                accum = accum + ridge
            for inner_index in range(row_index):
                accum = accum - upper[inner_index][row_index] * upper[inner_index][col_index]
            if row_index == col_index:
                upper[row_index][row_index] = jnp.sqrt(accum)
            else:
                upper[row_index][col_index] = accum / upper[row_index][row_index]
    listed = jnp.stack([upper[pair[0]][pair[1]] for pair in PAIR_LIST])
    inverse_list = jnp.stack([1.0 / upper[pair[0]][pair[1]] if pair[0] == pair[1] else upper[pair[0]][pair[1]] for pair in PAIR_LIST])
    spread = spread_blocks(inverse_list, blocks.shape[3])
    lookup = {}
    for position, pair in enumerate(PAIR_LIST):
        lookup[pair] = spread[position]
    columns = []
    for col_index in range(4):
        accum = blocks[col_index]
        for inner_index in range(col_index):
            accum = accum - lookup[inner_index, col_index] * columns[inner_index]
        columns.append(accum * lookup[col_index, col_index])
    return (jnp.stack(columns), listed)

def reference(test_vectors, conductivity):
    coef_pad = jnp.pad(conductivity, ((1, 1), (1, 1), (0, 0)), mode='wrap')
    widths = ((0, 0), (1, 1), (1, 1), (0, 0))
    first = sweep(jnp.pad(test_vectors, widths, mode='wrap'), coef_pad)
    relaxed = sweep(jnp.pad(first, widths, mode='wrap'), coef_pad)
    totals = lax.optimization_barrier(jnp.sum(relaxed * relaxed, axis=(1, 2, 3)))
    scales = lax.rsqrt(totals / (NZ * NY * NX) + 1e-06)
    normalized = relaxed * scales[:, None, None, None]
    rolled = jnp.roll(normalized, (-2, -2, -2), axis=(1, 2, 3))
    slabs = jnp.moveaxis(rolled.reshape(4, NZ // 4, 4, NY, NX), 1, 0)

    def one_slab(slab):
        return factor(slab, block_sums(pair_products(slab)))
    prolong, listed = lax.map(one_slab, slabs)
    prolong = jnp.moveaxis(prolong, 0, 1).reshape(4, NZ, NY, NX)
    prolong = jnp.roll(prolong, (2, 2, 2), axis=(1, 2, 3))
    factors = jnp.moveaxis(listed[:, :, 0], 0, 1)
    return (prolong, factors)
```

```python
import functools
import jax
import jax.numpy as jnp
from jax import lax
from jax.experimental import pallas as pl
from jax.experimental.pallas import tpu as pltpu
from jax.sharding import PartitionSpec as P

RELAX_WEIGHT = 2.0 / 3.0
PAIRS = ((0, 0), (0, 1), (0, 2), (0, 3), (1, 1), (1, 2), (1, 3), (2, 2), (2, 3), (3, 3))
AT = {pair: k for k, pair in enumerate(PAIRS)}
BLOCK = 4
EDGE = 8
VMEM_LIMIT = 40 * 1024 * 1024


def call(body, ins, outs, scratch=(), flops=0):
    names_in, names_out = list(ins), list(outs)

    def kernel(*refs):
        cut = len(names_in) + len(names_out)
        body(dict(zip(names_in, refs)), dict(zip(names_out, refs[len(names_in) :])), *refs[cut:])

    got = pl.pallas_call(
        kernel,
        out_shape=[jax.ShapeDtypeStruct(outs[k], jnp.float32) for k in names_out],
        in_specs=[pl.BlockSpec(memory_space=pltpu.VMEM)] * len(names_in),
        out_specs=[pl.BlockSpec(memory_space=pltpu.VMEM)] * len(names_out),
        scratch_shapes=list(scratch),
        compiler_params=pltpu.CompilerParams(vmem_limit_bytes=VMEM_LIMIT),
        cost_estimate=pl.CostEstimate(flops=flops, bytes_accessed=flops, transcendentals=0),
        name=body.__name__,
    )(*[ins[k] for k in names_in])
    return dict(zip(names_out, got))


def parity():
    return lax.rem(lax.axis_index("gz"), 2)


def natural(k, odd, planes):
    return k + odd * (planes - 1 - 2 * k)


def half_of_tile(shape):
    return lax.broadcasted_iota(jnp.int32, shape, 0) // BLOCK


def source(i, f, k, start, size, odd):
    planes = i["coef"].shape[0]
    rows = pl.ds(pl.multiple_of(start, 8), size)
    if f == i["tv"].shape[0]:
        return i["coef"][natural(k, odd, planes), rows, :]
    return i["tv"][f, natural(k, odd, planes), rows, :]


def pack_send(i, o):
    odd = parity()
    fields, planes, rows, width = i["tv"].shape
    half = rows // 2
    for k in range(2):
        for f in range(fields + 1):
            o["far"][k, f] = source(i, f, k, (1 - odd) * half, half, odd)
    which = half_of_tile((EDGE, width))
    for name, start, side in (
        ("extra", half - EDGE * (1 - odd), 1 - odd),
        ("halo", (rows - EDGE) * (1 - odd), 1 - odd),
        ("cross", (rows - EDGE) * odd, odd),
    ):
        for q in range(planes // 2):
            for f in range(fields + 1):
                u = source(i, f, 2 * q, start, EDGE, odd)
                v = source(i, f, 2 * q + 1, start, EDGE, odd)
                o[name][q, f] = jnp.where(which == side, u, pltpu.roll(v, BLOCK, 0))


def pack_keep(i, o):
    odd = parity()
    fields, planes, rows, width = i["tv"].shape
    half = rows // 2
    for k in range(planes):
        for f in range(fields + 1):
            o["far" if k < 2 else "near"][k % 2, f] = source(i, f, k, odd * half, half, odd)
            if k >= 2:
                o["send"][k % 2, f] = source(i, f, k, (1 - odd) * half, half, odd)


def edges(i, o):
    odd = parity()
    fields, planes, rows, width = i["tv"].shape
    half = rows // 2
    which = half_of_tile((EDGE, width))
    for k in range(planes):
        for f in range(fields + 1):

            def unpack(ref):
                tile = ref[k // 2, f]
                return tile if k % 2 == 0 else pltpu.roll(tile, BLOCK, 0)

            own = source(i, f, k, half - EDGE * odd, EDGE, odd)
            o["own_far" if k < 2 else "own_near"][k % 2, f] = jnp.where(which == odd, own, unpack(i["halo"]))
            o["par_far" if k < 2 else "par_near"][k % 2, f] = jnp.where(
                which == odd, unpack(i["extra"]), unpack(i["cross"])
            )


def inverse(x):
    guess = pl.reciprocal(x, approx=True)
    return guess * (2.0 - x * guess)


def onward(x, axis):
    return pltpu.roll(x, x.shape[axis] - 1, axis)


def backward(x, axis):
    return pltpu.roll(x, 1, axis)


def joint(a, b):
    return a * b * inverse(a + b)


def weigh(before, here, after, c):
    wx = joint(here, onward(here, 1))
    wy = joint(here, onward(here, 0))
    wm = joint(here, before)
    wp = joint(here, after)
    c[0] = wx
    c[1] = wy
    c[2] = wm
    c[3] = wp
    c[4] = RELAX_WEIGHT * inverse(wx + backward(wx, 1) + wy + backward(wy, 0) + wm + wp)


def step(before, here, after, c):
    fx = c[0] * (here - onward(here, 1))
    fy = c[1] * (here - onward(here, 0))
    flux = (fx - backward(fx, 1)) + (fy - backward(fy, 0))
    flux = flux + c[2] * (here - before) + c[3] * (here - after)
    return here - c[4] * flux


def window(keep, edge, at):
    return lambda f: jnp.concatenate([keep[at, f], edge[at, f]], axis=0)


def sweep_first(planes, z, c, out):
    last = 4
    weigh(planes[z - 1](last), planes[z](last), planes[z + 1](last), c)
    for f in range(last):
        out[f] = step(planes[z - 1](f), planes[z](f), planes[z + 1](f), c)


def sweep_second(first, z, c, keep, edge, at):
    half = keep.shape[2]
    for f in range(first[z].shape[0]):
        value = step(first[z - 1][f], first[z][f], first[z + 1][f], c)
        keep[at, f] = value[:half]
        edge[at, f] = value[half:]


def early(i, o):
    planes = {k: window(i["far"], i["far_edge"], k) for k in (0, 1)}
    planes |= {k + 2: window(i["near"], i["near_edge"], k) for k in (0, 1)}
    sweep_first(planes, 1, o["c1"], o["f1"])
    sweep_first(planes, 2, o["c2"], o["f2"])


def outer(i, o, c8):
    planes = {7 - k: window(i["far"], i["far_edge"], k) for k in (0, 1)}
    planes |= {8 + k: window(i["next"], i["next_edge"], k) for k in (0, 1)}
    sweep_first(planes, 7, o["c7"], o["f7"])
    sweep_first(planes, 8, c8, o["f8"])


def inner_far(i, o, c6):
    planes = {7 - k: window(i["far"], i["far_edge"], k) for k in (0, 1)}
    planes |= {5 - k: window(i["near"], i["near_edge"], k) for k in (0, 1)}
    sweep_first(planes, 6, c6, o["f6"])
    sweep_first(planes, 5, o["c5"], o["f5"])
    first = {5: o["f5"], 6: o["f6"], 7: i["f7"], 8: i["f8"]}
    sweep_second(first, 7, i["c7"], o["rel"], o["rel_edge"], 0)
    sweep_second(first, 6, c6, o["rel"], o["rel_edge"], 1)


def inner_near(i, o, c4):
    planes = {2 + k: window(i["own"], i["own_edge"], k) for k in (0, 1)}
    planes |= {5 - k: window(i["near"], i["near_edge"], k) for k in (0, 1)}
    sweep_first(planes, 4, c4, o["f4"])
    sweep_first(planes, 3, o["c3"], o["f3"])
    first = {3: o["f3"], 4: o["f4"], 5: i["f5"], 6: i["f6"]}
    sweep_second(first, 5, i["c5"], o["rel"], o["rel_edge"], 0)
    sweep_second(first, 4, c4, o["rel"], o["rel_edge"], 1)


def split(x):
    high = x.astype(jnp.bfloat16)
    return high, (x - high.astype(jnp.float32)).astype(jnp.bfloat16)


def times_table(x, table):
    high, low = split(x)
    return jnp.dot(high, table, preferred_element_type=jnp.float32) + jnp.dot(
        low, table, preferred_element_type=jnp.float32
    )


def table_times(table, x):
    high, low = split(x)
    return jnp.dot(table, high, preferred_element_type=jnp.float32) + jnp.dot(
        table, low, preferred_element_type=jnp.float32
    )


def lane_table(width, transposed=False):
    shape = (width // BLOCK, width) if transposed else (width, width // BLOCK)
    cell = lax.broadcasted_iota(jnp.int32, shape, 1 if transposed else 0)
    block = lax.broadcasted_iota(jnp.int32, shape, 0 if transposed else 1)
    moved = jnp.where(cell < 2, cell + width - 2, cell - 2)
    return (moved // BLOCK == block).astype(jnp.bfloat16)


def row_table(half, groups):
    shape = (groups, half + EDGE)
    row = lax.broadcasted_iota(jnp.int32, shape, 1)
    block = lax.broadcasted_iota(jnp.int32, shape, 0)
    moved = jnp.where(row >= half + EDGE - 2, row - (half + EDGE - 2), row + 2)
    return ((moved // BLOCK == block) & (block <= half // BLOCK)).astype(jnp.bfloat16)


def group_count(half):
    return (half // BLOCK + 1 + 7) // 8 * 8


def grams(planes, out, sums, half):
    width = out.shape[-1] * BLOCK
    lanes, rows = lane_table(width), row_table(half, out.shape[1])
    for at, (a, b) in enumerate(PAIRS):
        total = None
        for keep, edge, k in planes:
            left = jnp.concatenate([keep[k, a], edge[k, a]], axis=0)
            right = left if a == b else jnp.concatenate([keep[k, b], edge[k, b]], axis=0)
            total = left * right if total is None else total + left * right
        if a == b:
            kept = jnp.sum(total[:half], axis=0, keepdims=True)
            sums[a : a + 1] = sums[a : a + 1] + kept[:, : width // 2] + kept[:, width // 2 :]
        out[at] = table_times(rows, times_table(total, lanes))


def middle(i, o):
    first = {k: i[f"f{k}"] for k in (1, 2, 3, 4)}
    sweep_second(first, 2, i["c2"], o["rel"], o["rel_edge"], 0)
    sweep_second(first, 3, i["c3"], o["rel"], o["rel_edge"], 1)
    half = o["rel"].shape[2]
    o["sums"][...] = jnp.zeros_like(o["sums"])
    near = [(o["rel"], o["rel_edge"], k) for k in (0, 1)] + [(i["pn"], i["pn_edge"], k) for k in (0, 1)]
    grams([(i["pf"], i["pf_edge"], k) for k in (0, 1)], o["gram"].at[0], o["sums"], half)
    grams(near, o["gram"].at[1], o["sums"], half)


def outmost(i, o, cm, c0, fm, f0):
    planes = {-1 - k: window(i["prev"], i["prev_edge"], k) for k in (0, 1)}
    planes |= {k: window(i["far"], i["far_edge"], k) for k in (0, 1)}
    sweep_first(planes, -1, cm, fm)
    sweep_first(planes, 0, c0, f0)
    first = {-1: fm, 0: f0, 1: i["f1"], 2: i["f2"]}
    sweep_second(first, 0, c0, o["rel"], o["rel_edge"], 0)
    sweep_second(first, 1, i["c1"], o["rel"], o["rel_edge"], 1)
    o["sums"][...] = i["sums"][...]
    grams([(o["rel"], o["rel_edge"], k) for k in (0, 1)], o["gram"], o["sums"], o["rel"].shape[2])


def finish(cells, i, o, spread):
    odd = parity()
    fields, planes, rows, width = o["prolong"].shape
    half = rows // 2
    totals = jnp.sum(jnp.sum(i["totals"][...], axis=0), axis=1, keepdims=True)
    scales = lax.rsqrt(totals / cells + 1e-06)
    scale = [jnp.broadcast_to(scales[f : f + 1], (1, 1)) for f in range(fields)]
    groups = i["own_far"].shape[1]
    matrix = {}
    for at, (a, b) in enumerate(PAIRS):
        stacked = jnp.concatenate(
            [
                i["own_far"][at] + i["same"][at],
                i["own"][1, at],
                i["other"][0, at] + i["cross"][at],
                i["other"][1, at],
            ],
            axis=0,
        )
        matrix[a, b] = stacked * (scale[a] * scale[b])
    trace = matrix[0, 0] + matrix[1, 1] + matrix[2, 2] + matrix[3, 3]
    ridge = 0.64 * (trace / 256.0 + 1e-06)
    upper, inv = {}, {}
    for a in range(fields):
        for b in range(a, fields):
            accum = matrix[a, b] + ridge if a == b else matrix[a, b]
            for c in range(a):
                accum = accum - upper[c, a] * upper[c, b]
            if a == b:
                upper[a, a] = jnp.sqrt(accum)
                inv[a] = 1.0 / upper[a, a]
            else:
                upper[a, b] = accum * inv[a]
    count = rows // BLOCK
    line = lax.broadcasted_iota(jnp.int32, (count, width // BLOCK), 0)
    lanes = lane_table(width, True)
    for at, (a, b) in enumerate(PAIRS):
        value = upper[a, b]
        part = [value[n * groups : (n + 1) * groups] for n in range(4)]
        pad = jnp.zeros((count - groups, width // BLOCK), jnp.float32)
        low = jnp.concatenate([jnp.where(odd == 0, part[1], part[2]), pad], axis=0)
        top = jnp.concatenate([jnp.where(odd == 0, part[3], part[0]), pad], axis=0)
        low, top = onward(low, 0), pltpu.roll(top, half // BLOCK - 1, 0)
        o["factors"][at, 0] = jnp.where(line < half // BLOCK, low, top)
        spread[at] = times_table(inv[a] if a == b else value, lanes)
    within = lax.broadcasted_iota(jnp.int32, (EDGE, width), 0)
    for side in range(2):
        start = (odd if side == 0 else 1 - odd) * half
        for pair in range(2):
            source_ref = i[("near" if pair else "far") if side == 0 else ("back_near" if pair else "back_far")]
            base = (2 * side + pair) * groups
            for tile in range(half // EDGE):
                entry = {}
                for at, key in enumerate(PAIRS):
                    three = [
                        jnp.broadcast_to(spread[at, pl.ds(base + 2 * tile + n, 1), :], (EDGE, width)) for n in range(3)
                    ]
                    entry[key] = jnp.where(within < 2, three[0], jnp.where(within < 6, three[1], three[2]))
                for k in range(2):
                    columns = []
                    for b in range(fields):
                        accum = source_ref[k, b, pl.ds(tile * EDGE, EDGE), :] * scale[b]
                        for a in range(b):
                            accum = accum - entry[a, b] * columns[a]
                        columns.append(accum * entry[b, b])
                        place = pl.ds(pl.multiple_of(start + tile * EDGE, 8), EDGE)
                        o["prolong"][b, natural(2 * pair + k, odd, planes), place, :] = columns[b]


def moved(x, even_by, odd_by):
    nz, ny = lax.axis_size("gz"), lax.axis_size("gy")
    route = []
    for z in range(nz):
        dz, dy = odd_by if z % 2 else even_by
        for y in range(ny):
            route.append((z * ny + y, (z + dz) % nz * ny + (y + dy) % ny))
    return lax.ppermute(x, ("gz", "gy"), route)


def body(tv, coef):
    fields, planes, rows, width = tv.shape
    half = rows // 2
    devices = lax.axis_size("gz") * lax.axis_size("gy")
    cells = devices * planes * rows * width
    groups = group_count(half)
    keep = (2, fields + 1, half, width)
    edge = (2, fields + 1, EDGE, width)
    tall = half + EDGE
    first, coefs = (fields, tall, width), (5, tall, width)
    rel, rel_edge = (2, fields, half, width), (2, fields, EDGE, width)
    gram = (len(PAIRS), groups, width // BLOCK)
    sums = (8, width // 2)

    send = call(pack_send, dict(tv=tv, coef=coef), dict(far=keep, extra=edge, halo=edge, cross=edge))
    par_far = moved(send["far"], (1, 0), (-1, 0))
    extra = moved(send["extra"], (1, 0), (-1, 0))
    cross = moved(send["cross"], (1, -1), (-1, 1))
    halo = moved(send["halo"], (0, 1), (0, -1))
    own = call(pack_keep, dict(tv=tv, coef=coef), dict(far=keep, near=keep, send=keep))
    par_near = moved(own["send"], (1, 0), (-1, 0))
    after = moved(own["far"], (-2, 0), (2, 0))
    e = call(
        edges,
        dict(tv=tv, coef=coef, extra=extra, halo=halo, cross=cross),
        dict(own_far=edge, own_near=edge, par_far=edge, par_near=edge),
    )
    after_edge = moved(e["own_far"], (-2, 0), (2, 0))
    before = moved(par_far, (2, 0), (-2, 0))
    before_edge = moved(e["par_far"], (2, 0), (-2, 0))
    a = call(
        early,
        dict(far=own["far"], far_edge=e["own_far"], near=own["near"], near_edge=e["own_near"]),
        dict(c1=coefs, c2=coefs, f1=first, f2=first),
    )
    b = call(
        outer,
        dict(far=par_far, far_edge=e["par_far"], next=after, next_edge=after_edge),
        dict(c7=coefs, f7=first, f8=first),
        [pltpu.VMEM(coefs, jnp.float32)],
    )
    far = call(
        inner_far,
        dict(far=par_far, far_edge=e["par_far"], near=par_near, near_edge=e["par_near"], **b),
        dict(c5=coefs, f5=first, f6=first, rel=rel, rel_edge=rel_edge),
        [pltpu.VMEM(coefs, jnp.float32)],
    )
    back_far = moved(far["rel"], (1, 0), (-1, 0))
    near = call(
        inner_near,
        dict(
            own=own["near"],
            own_edge=e["own_near"],
            near=par_near,
            near_edge=e["par_near"],
            c5=far["c5"],
            f5=far["f5"],
            f6=far["f6"],
        ),
        dict(c3=coefs, f3=first, f4=first, rel=rel, rel_edge=rel_edge),
        [pltpu.VMEM(coefs, jnp.float32)],
    )
    back_near = moved(near["rel"], (1, 0), (-1, 0))
    mid = call(
        middle,
        dict(
            f1=a["f1"],
            f2=a["f2"],
            f3=near["f3"],
            f4=near["f4"],
            c2=a["c2"],
            c3=near["c3"],
            pf=far["rel"],
            pf_edge=far["rel_edge"],
            pn=near["rel"],
            pn_edge=near["rel_edge"],
        ),
        dict(rel=rel, rel_edge=rel_edge, gram=(2,) + gram, sums=sums),
    )
    other = moved(mid["gram"], (1, 0), (-1, 0))
    same = moved(mid["gram"][0], (2, 0), (-2, 0))
    out = call(
        outmost,
        dict(
            prev=before,
            prev_edge=before_edge,
            far=own["far"],
            far_edge=e["own_far"],
            f1=a["f1"],
            f2=a["f2"],
            c1=a["c1"],
            sums=mid["sums"],
        ),
        dict(rel=rel, rel_edge=rel_edge, gram=gram, sums=sums),
        [pltpu.VMEM(coefs, jnp.float32)] * 2 + [pltpu.VMEM(first, jnp.float32)] * 2,
    )
    crossed = moved(out["gram"], (-1, 0), (1, 0))
    totals = lax.all_to_all(jnp.broadcast_to(out["sums"], (devices,) + sums), ("gz", "gy"), 0, 0)
    final = functools.partial(finish, float(cells))
    final.__name__ = "finish"
    done = call(
        final,
        dict(
            totals=totals,
            own_far=out["gram"],
            same=same,
            own=mid["gram"],
            other=other,
            cross=crossed,
            far=out["rel"],
            near=mid["rel"],
            back_far=back_far,
            back_near=back_near,
        ),
        dict(prolong=tv.shape, factors=(len(PAIRS), planes // BLOCK, rows // BLOCK, width // BLOCK)),
        [pltpu.VMEM((len(PAIRS), 4 * groups, width), jnp.float32)],
    )
    return done["prolong"], done["factors"]


def solution(mesh):
    return jax.shard_map(
        body,
        mesh=mesh,
        in_specs=(P(None, "gz", "gy", None), P("gz", "gy", None)),
        out_specs=(P(None, "gz", "gy", None), P(None, "gz", "gy", None)),
        check_vma=False,
    )
```

```python
import functools
import types
import jax
import jax.numpy as jnp
from jax import lax
from jax.experimental import pallas as pl
from jax.experimental.pallas import tpu as pltpu
from jax.sharding import PartitionSpec as P

RELAX_WEIGHT = 2.0 / 3.0
PAIRS = ((0, 0), (0, 1), (0, 2), (0, 3), (1, 1), (1, 2), (1, 3), (2, 2), (2, 3), (3, 3))
AT = {pair: k for k, pair in enumerate(PAIRS)}
BLOCK = 4
EDGE = 8
VMEM_LIMIT = 40 * 1024 * 1024

COST = {'inner': 10, 'pack_near': 8}


def call(body, ins, outs, scratch=(), far=(), alias=None):
    names_in, names_out = list(ins), list(outs)

    def kernel(*refs):
        cut = len(names_in) + len(names_out)
        i = types.SimpleNamespace(**dict(zip(names_in, refs)))
        o = types.SimpleNamespace(**dict(zip(names_out, refs[len(names_in) :])))
        body(i, o, *refs[cut:])

    def spec(name):
        return pl.BlockSpec(memory_space=pltpu.HBM if name in far else pltpu.VMEM)

    got = pl.pallas_call(
        kernel,
        out_shape=[jax.ShapeDtypeStruct(outs[k], jnp.float32) for k in names_out],
        in_specs=[spec(k) for k in names_in],
        out_specs=[spec(k) for k in names_out],
        scratch_shapes=list(scratch),
        input_output_aliases={names_in.index(a): names_out.index(b) for a, b in (alias or {}).items()},
        compiler_params=pltpu.CompilerParams(vmem_limit_bytes=VMEM_LIMIT),
        cost_estimate=pl.CostEstimate(flops=int(COST.get(body.__name__, 0) * 1e9), bytes_accessed=0, transcendentals=0),
        name=body.__name__,
    )(*[ins[k] for k in names_in])
    return types.SimpleNamespace(**dict(zip(names_out, got)))


def parity():
    return lax.rem(lax.axis_index("gz"), 2)


def natural(k, odd, planes):
    return k + odd * (planes - 1 - 2 * k)


def half_of_tile(shape):
    return lax.broadcasted_iota(jnp.int32, shape, 0) // BLOCK


def rows_at(start, size):
    return pl.ds(pl.multiple_of(start, 8), size)


def copies(jobs, sems):
    started = [pltpu.make_async_copy(a, b, sems.at[n]) for n, (a, b) in enumerate(jobs)]
    for one in started:
        one.start()
    return started


def plane_jobs(i, k, odd, start, target):
    fields, planes = i.tv.shape[:2]
    half = i.tv.shape[2] // 2
    at, rows = natural(k, odd, planes), rows_at(start, half)
    return [
        (i.tv.at[:, at, rows, :], target.at[pl.ds(0, fields), pl.ds(0, half), :]),
        (i.coef.at[at, rows, :], target.at[fields, pl.ds(0, half), :]),
    ]


def tile_jobs(i, start, target):
    fields, rows = i.tv.shape[0], rows_at(start, EDGE)
    return [
        (i.tv.at[:, :, rows, :], target.at[pl.ds(0, fields)]),
        (i.coef.at[:, rows, :], target.at[fields]),
    ]


def packed(tiles, q, f, side, odd, which):
    planes = tiles.shape[1]
    u, v = tiles[f, natural(2 * q, odd, planes)], tiles[f, natural(2 * q + 1, odd, planes)]
    return jnp.where(which == side, u, pltpu.roll(v, BLOCK, 0))


def unpacked(tile, k):
    return tile if k % 2 == 0 else pltpu.roll(tile, BLOCK, 0)


def pack_first(i, o, extra, halo, cross, edge, sems, late_sems):
    odd = parity()
    fields, planes, rows, width = i.tv.shape
    half = rows // 2
    jobs = tile_jobs(i, half - EDGE * (1 - odd), extra)
    jobs += tile_jobs(i, (rows - EDGE) * (1 - odd), halo) + tile_jobs(i, (rows - EDGE) * odd, cross)
    jobs += plane_jobs(i, 0, odd, (1 - odd) * half, o.far0)
    for k in range(2):
        jobs += plane_jobs(i, k, odd, odd * half, o.own.at[k])
    started = copies(jobs, sems)
    for one in started[:6]:
        one.wait()
    which = half_of_tile((EDGE, width))
    for q in range(planes // 2):
        for f in range(fields + 1):
            edge[q, f] = packed(extra, q, f, 1 - odd, odd, which)
            o.halo[q, f] = packed(halo, q, f, 1 - odd, odd, which)
            o.cross[q, f] = packed(cross, q, f, odd, odd, which)
    more = [(edge.at[q], o.far0.at[:, pl.ds(half + q * EDGE, EDGE), :]) for q in range(planes // 2)]
    for one in started[6:] + copies(more, late_sems):
        one.wait()


def pack_second(i, o, extra, sems):
    odd = parity()
    fields, planes, rows, width = i.tv.shape
    half = rows // 2
    jobs = tile_jobs(i, half - EDGE * odd, extra)
    jobs += plane_jobs(i, 1, odd, (1 - odd) * half, o.far1)
    for k in range(2):
        jobs += plane_jobs(i, 2 + k, odd, odd * half, o.near.at[k])
    started = copies(jobs, sems)
    o.far[:, :, :half] = i.own[...]
    for q in range(planes // 2):
        o.far1[:, pl.ds(half + q * EDGE, EDGE), :] = i.cross[q]
    for one in started:
        one.wait()
    which = half_of_tile((EDGE, width))
    for k in range(planes):
        for f in range(fields + 1):
            own = extra[f, natural(k, odd, planes)]
            window_of = (o.far if k < 2 else o.near)
            tile = jnp.where(which == odd, own, unpacked(i.halo[k // 2, f], k))
            window_of[k % 2, f, half:] = tile
            if k < 2:
                o.far_edge[k, f] = tile


def pack_near(i, o, sems):
    odd = parity()
    half = i.tv.shape[2] // 2
    jobs = []
    for k in range(2):
        jobs += plane_jobs(i, 2 + k, odd, (1 - odd) * half, (o.send1 if k else o.send0))
    started = copies(jobs, sems)
    o.on[...] = i.far0[:, :half]
    for one in started:
        one.wait()


def pack_third(i, o):
    odd = parity()
    fields, tall, width = i.far0.shape
    half = tall - 2 * EDGE
    which = half_of_tile((EDGE, width))
    for k in range(4):
        for f in range(fields):
            extra = i.far0[f, pl.ds(half + k // 2 * EDGE, EDGE), :]
            cross = i.far1[f, pl.ds(half + k // 2 * EDGE, EDGE), :]
            tile = jnp.where(which == odd, unpacked(extra, k), unpacked(cross, k))
            if k < 2:
                plane = (i.far1 if k else i.far0)[f, :half]
                o.far[k, f, :half] = plane
                o.far[k, f, half:] = tile
                o.send[f, pl.ds(half + (1 - k) * EDGE, EDGE), :] = tile
                if k == 1:
                    o.send[f, :half] = plane
            else:
                o.near_edge[k - 2, f] = tile


def inverse(x):
    guess = pl.reciprocal(x, approx=True)
    return guess * (2.0 - x * guess)


def onward(x, axis):
    return pltpu.roll(x, x.shape[axis] - 1, axis)


def backward(x, axis):
    return pltpu.roll(x, 1, axis)


def joint(a, b):
    return a * b * inverse(a + b)


def weigh(before, here, after, c):
    wx = joint(here, onward(here, 1))
    wy = joint(here, onward(here, 0))
    wm = joint(here, before)
    wp = joint(here, after)
    c[0] = wx
    c[1] = wy
    c[2] = wm
    c[3] = wp
    c[4] = RELAX_WEIGHT * inverse(wx + backward(wx, 1) + wy + backward(wy, 0) + wm + wp)


def step(before, here, after, c):
    fx = c[0] * (here - onward(here, 1))
    fy = c[1] * (here - onward(here, 0))
    flux = (fx - backward(fx, 1)) + (fy - backward(fy, 0))
    flux = flux + c[2] * (here - before) + c[3] * (here - after)
    return here - c[4] * flux


def window(whole, at):
    return lambda f: whole[at, f]


def joined(keep, edge, at):
    return lambda f: jnp.concatenate([keep[f], edge[at, f]], axis=0)


def sweep_first(planes, z, c, out):
    last = 4
    weigh(planes[z - 1](last), planes[z](last), planes[z + 1](last), c)
    for f in range(last):
        out[f] = step(planes[z - 1](f), planes[z](f), planes[z + 1](f), c)


def sweep_second(first, z, c, keep, edge):
    half = keep.shape[1]
    for f in range(first[z].shape[0]):
        value = step(first[z - 1][f], first[z][f], first[z + 1][f], c)
        keep[f] = value[:half]
        edge[f] = value[half:]


def early(i, o):
    planes = {k: window(i.far, k) for k in (0, 1)} | {k + 2: window(i.near, k) for k in (0, 1)}
    sweep_first(planes, 1, o.c1, o.f1)
    sweep_first(planes, 2, o.c2, o.f2)


def outer(i, o, c8):
    planes = {7 - k: window(i.far, k) for k in (0, 1)}
    planes |= {8 + k: joined(i.next.at[k], i.next_edge, k) for k in (0, 1)}
    sweep_first(planes, 7, o.c7, o.f7)
    sweep_first(planes, 8, c8, o.f8)


def inner_last(i, o):
    planes = {7 - k: window(i.far, k) for k in (0, 1)} | {5: joined(i.near5, i.near_edge, 0)}
    sweep_first(planes, 6, o.c6, o.f6)
    sweep_second({6: o.f6, 7: i.f7, 8: i.f8}, 7, i.c7, o.rel, o.rel_edge)


def inner(i, o):
    planes = {3: window(i.own, 1), 6: window(i.far, 1)}
    planes |= {5 - k: joined((i.near4 if k else i.near5), i.near_edge, k) for k in (0, 1)}
    sweep_first(planes, 5, o.c5, o.f5)
    sweep_first(planes, 4, o.c4, o.f4)
    first = {4: o.f4, 5: o.f5, 6: i.f6, 7: i.f7}
    sweep_second(first, 6, i.c6, o.rel.at[0], o.rel_edge.at[0])
    sweep_second(first, 5, o.c5, o.rel.at[1], o.rel_edge.at[1])


def squares(refs, sums, before=None):
    fields, half, width = refs[0].shape
    for f in range(fields):
        total = jnp.zeros((EDGE, width), jnp.float32)
        for ref in refs:
            for tile in range(half // EDGE):
                part = ref[f, pl.ds(tile * EDGE, EDGE), :]
                total = total + part * part
        total = jnp.sum(total[:, : width // 2] + total[:, width // 2 :], axis=0, keepdims=True)
        sums[f : f + 1] = total if before is None else total + before[f : f + 1]


def near_rest(i, o, c3, f3):
    planes = {2 + k: window(i.near, k) for k in (0, 1)} | {4: joined(i.near4, i.near_edge, 1)}
    sweep_first(planes, 3, c3, f3)
    first = {1: i.f1, 2: i.f2, 4: i.f4, 5: i.f5} | {3: f3}
    sweep_second(first, 4, i.c4, o.rel4, o.rel4_edge)
    sweep_second(first, 2, i.c2, o.rel.at[0], o.rel_edge.at[0])
    sweep_second(first, 3, c3, o.rel.at[1], o.rel_edge.at[1])
    squares([o.rel4, o.rel.at[0], o.rel.at[1], i.rel7, i.rel.at[0], i.rel.at[1]], o.sums)


def far_rest(i, o, cm, c0, fm, f0, own_sums):
    planes = {k: window(i.far, k) for k in (0, 1)}
    tall = i.far.shape[2]
    planes[-1] = lambda f: jnp.concatenate([i.prev0[f], i.prev1[f, tall:]], axis=0)
    planes[-2] = lambda f: i.prev1[f, :tall]
    sweep_first(planes, -1, cm, fm)
    sweep_first(planes, 0, c0, f0)
    first = {-1: fm, 0: f0, 1: i.f1, 2: i.f2}
    sweep_second(first, 0, c0, o.rel.at[0], o.rel_edge.at[0])
    sweep_second(first, 1, i.c1, o.rel.at[1], o.rel_edge.at[1])
    squares([o.rel.at[0], o.rel.at[1]], own_sums, i.sums)
    for n in range(o.sums.shape[0]):
        o.sums[n] = own_sums[...]


def split(x):
    high = x.astype(jnp.bfloat16)
    return high, (x - high.astype(jnp.float32)).astype(jnp.bfloat16)


def times_table(x, table):
    high, low = split(x)
    return jnp.dot(high, table, preferred_element_type=jnp.float32) + jnp.dot(
        low, table, preferred_element_type=jnp.float32
    )


def lane_table(width, spread):
    part = width // BLOCK
    shape = (part, width) if spread else (width, part)
    cell = lax.broadcasted_iota(jnp.int32, shape, 1 if spread else 0)
    block = lax.broadcasted_iota(jnp.int32, shape, 0 if spread else 1)
    moved = jnp.where(cell < 2, cell + width - 2, cell - 2)
    return (moved // BLOCK == block).astype(jnp.bfloat16)


def group_count(half):
    return (half // BLOCK + 1 + 7) // 8 * 8


def grams(planes, out, stacked, folded):
    half, width = planes[0][0].shape[1:]
    tall, part, groups = half + EDGE, width // BLOCK, group_count(half)
    for at, (a, b) in enumerate(PAIRS):
        total = None
        for keep, edge in planes:
            left = jnp.concatenate([keep[a], edge[a]], axis=0)
            right = left if a == b else jnp.concatenate([keep[b], edge[b]], axis=0)
            total = left * right if total is None else total + left * right
        stacked[pl.ds(at * tall, tall), :] = total
    across = times_table(stacked[...], lane_table(width, False))
    for at in range(len(PAIRS)):
        two = across[at * tall : (at + 1) * tall]
        two = two + backward(two, 0)
        folded[at, :tall] = two + pltpu.roll(two, 2, 0)
        folded[at, tall:] = jnp.zeros((groups * BLOCK - tall, part), jnp.float32)
    for at in range(len(PAIRS)):
        value = folded[at, pl.ds(1, groups, stride=BLOCK), :]
        out[pl.ds(at // BLOCK * groups, groups), pl.ds(at % BLOCK * part, part)] = value


def products(i, o, stacked, folded):
    rel4 = (i.rel4, i.rel4_edge)
    far, near = [(i.rel.at[k], i.rel_edge.at[k]) for k in range(2)]
    own = [(i.own.at[k], i.own_edge.at[k]) for k in range(2)]
    mid = [(i.mid.at[k], i.mid_edge.at[k]) for k in range(2)]
    count = o.far.shape[0]
    grams([(i.rel7, i.rel7_edge), far], o.far, stacked, folded)
    grams(own, o.gram, stacked, folded)
    grams(mid + [rel4, near], o.mid, stacked, folded)
    o.both[:count] = o.far[...]
    o.both[count:] = o.mid[...]


def solve_rows(rel, spread, base, scale, result, z):
    fields, half, width = result.shape[1:]
    rel = rel if isinstance(rel, list) else [rel.at[f] for f in range(fields)]
    within = lax.broadcasted_iota(jnp.int32, (EDGE, width), 0)
    for tile in range(half // EDGE):
        entry = {}
        for at, key in enumerate(PAIRS):
            three = [jnp.broadcast_to(spread[at, pl.ds(base + 2 * tile + n, 1), :], (EDGE, width)) for n in range(3)]
            entry[key] = jnp.where(within < 2, three[0], jnp.where(within < 6, three[1], three[2]))
        rows = pl.ds(tile * EDGE, EDGE)
        columns = []
        for b in range(fields):
            accum = rel[b][rows, :] * scale[b]
            for a in range(b):
                accum = accum - entry[a, b] * columns[a]
            columns.append(accum * entry[b, b])
            result[z, b, rows, :] = columns[b]


def write_plane(result, z, prolong, start, odd, sems):
    planes, half = prolong.shape[1], result.shape[2]
    target = prolong.at[:, natural(z, odd, planes), rows_at(start, half), :]
    one = pltpu.make_async_copy(result.at[z], target, sems.at[z])
    one.start()
    return one


def triangle(scale, values):
    fields = len(scale)
    matrix = {(a, b): values(at) * (scale[a] * scale[b]) for at, (a, b) in enumerate(PAIRS)}
    trace = matrix[0, 0] + matrix[1, 1] + matrix[2, 2] + matrix[3, 3]
    ridge = 0.64 * (trace / 256.0 + 1e-06)
    upper, inv = {}, {}
    for a in range(fields):
        for b in range(a, fields):
            accum = matrix[a, b] + ridge if a == b else matrix[a, b]
            for c in range(a):
                accum = accum - upper[c, a] * upper[c, b]
            if a == b:
                upper[a, a] = jnp.sqrt(accum)
                inv[a] = 1.0 / upper[a, a]
            else:
                upper[a, b] = accum * inv[a]
    return upper, inv


def spread_all(upper, inv, lanes, spread):
    entries = [inv[a] if a == b else upper[a, b] for a, b in PAIRS]
    rows = entries[0].shape[0]
    wide = times_table(jnp.concatenate(entries, axis=0), lanes)
    for at in range(len(PAIRS)):
        spread[at] = wide[at * rows : (at + 1) * rows]


def gram_at(ref, at, groups, start=0):
    part = ref.shape[-1] // BLOCK
    return ref[pl.ds(start + at // BLOCK * groups, groups), pl.ds(at % BLOCK * part, part)]


def finish_own(cells, i, o, result, spread, sems):
    odd = parity()
    fields, planes, rows, width = o.prolong.shape
    half = rows // 2
    groups = group_count(half)
    totals = jnp.sum(jnp.sum(i.totals[...], axis=0), axis=1, keepdims=True)
    scales = lax.rsqrt(totals / cells + 1e-06)
    o.scales[...] = jnp.broadcast_to(scales, o.scales.shape)
    scale = [scales[f : f + 1] for f in range(fields)]
    upper, inv = triangle(
        scale,
        lambda at: jnp.concatenate(
            [gram_at(i.gram, at, groups) + gram_at(i.same, at, groups), gram_at(i.mid, at, groups)], axis=0
        ),
    )
    lanes = lane_table(width, True)
    for at, (a, b) in enumerate(PAIRS):
        value = upper[a, b]
        o.mine[at] = jnp.where(odd == 0, value[groups:], value[:groups])
    spread_all(upper, inv, lanes, spread)
    writes = []
    for z in range(planes):
        solve_rows((i.far if z < 2 else i.near).at[z % 2], spread, z // 2 * groups, scale, result, z)
        writes.append(write_plane(result, z, o.prolong, odd * half, odd, sems))
    for one in writes:
        one.wait()


def finish_other(i, o, result, spread, sems):
    odd = parity()
    fields, planes, rows, width = o.prolong.shape
    half = rows // 2
    groups = group_count(half)
    scale = [i.scales[f : f + 1, :1] for f in range(fields)]
    both = i.both
    mid_start = i.cross.shape[0]
    upper, inv = triangle(
        scale,
        lambda at: jnp.concatenate(
            [gram_at(both, at, groups) + gram_at(i.cross, at, groups), gram_at(both, at, groups, mid_start)],
            axis=0,
        ),
    )
    lanes = lane_table(width, True)
    count = rows // BLOCK
    line = lax.broadcasted_iota(jnp.int32, (count, width // BLOCK), 0)
    pad = jnp.zeros((count - groups, width // BLOCK), jnp.float32)
    for at, (a, b) in enumerate(PAIRS):
        value = upper[a, b]
        mine, theirs = i.mine[at], jnp.where(odd == 0, value[groups:], value[:groups])
        low = jnp.concatenate([jnp.where(odd == 0, mine, theirs), pad], axis=0)
        top = jnp.concatenate([jnp.where(odd == 0, theirs, mine), pad], axis=0)
        low, top = onward(low, 0), pltpu.roll(top, half // BLOCK - 1, 0)
        o.factors[at, 0] = jnp.where(line < half // BLOCK, low, top)
    spread_all(upper, inv, lanes, spread)
    writes = []
    for z in range(planes):
        rel = i.last if z == 0 else i.back.at[z - 1] if z < planes - 1 else i.back4
        solve_rows(rel, spread, z // 2 * groups, scale, result, z)
        writes.append(write_plane(result, z, o.prolong, (1 - odd) * half, odd, sems))
    for one in writes:
        one.wait()


def moved(name, x, even_by, odd_by):
    nz, ny = lax.axis_size("gz"), lax.axis_size("gy")
    route = []
    for z in range(nz):
        dz, dy = odd_by if z % 2 else even_by
        for y in range(ny):
            route.append((z * ny + y, (z + dz) % nz * ny + (y + dy) % ny))
    with jax.named_scope(name):
        return lax.ppermute(x, ("gz", "gy"), route)


def body(tv, coef):
    fields, planes, rows, width = tv.shape
    half = rows // 2
    devices = lax.axis_size("gz") * lax.axis_size("gy")
    cells = devices * planes * rows * width
    groups = group_count(half)
    tall = half + EDGE
    windows, edge = (2, fields + 1, tall, width), (2, fields + 1, EDGE, width)
    keep, keeps = (fields + 1, half, width), (2, fields + 1, half, width)
    first, coefs = (fields, tall, width), (5, tall, width)
    gram = (-(-len(PAIRS) // BLOCK) * groups, width)
    sums = (8, width // 2)
    rel, rel_edge = (fields, half, width), (fields, EDGE, width)

    def local(shape):
        return pltpu.VMEM(shape, jnp.float32)

    tiles = local((fields + 1, planes, EDGE, width))
    args = dict(tv=tv, coef=coef)
    sent = call(
        pack_first,
        args,
        dict(far0=(fields + 1, half + 2 * EDGE, width), own=keeps, halo=edge, cross=edge),
        [tiles] * 3 + [local(edge), pltpu.SemaphoreType.DMA((12,)), pltpu.SemaphoreType.DMA((2,))],
        far=("tv", "coef"),
    )
    far0 = moved("far0", sent.far0, (1, 0), (-1, 0))
    halo = moved("halo", sent.halo, (0, 1), (0, -1))
    cross = moved("cross", sent.cross, (0, -1), (0, 1))
    after = moved("after", sent.own, (-2, 0), (2, 0))
    own = call(
        pack_second,
        dict(halo=halo, cross=cross, own=sent.own, **args),
        dict(
            far=windows,
            near=windows,
            far1=(fields + 1, half + 2 * EDGE, width),
            far_edge=edge,
        ),
        [tiles, pltpu.SemaphoreType.DMA((8,))],
        far=("tv", "coef"),
    )
    to_near = call(
        pack_near,
        dict(far0=far0, **args),
        dict(send0=keep, send1=keep, on=keep),
        [pltpu.SemaphoreType.DMA((4,))],
        far=("tv", "coef"),
    )
    prev0 = moved("prev0", to_near.on, (2, 0), (-2, 0))
    far1 = moved("far1", own.far1, (1, 0), (-1, 0))
    near5 = moved("near5", to_near.send0, (1, 0), (-1, 0))
    near4 = moved("near4", to_near.send1, (1, 0), (-1, 0))
    after_edge = moved("after_edge", own.far_edge, (-2, 0), (2, 0))
    a = call(
        early,
        dict(far=own.far, near=own.near, gate=after_edge),
        dict(c1=coefs, c2=coefs, f1=first, f2=first),
    )
    par = call(
        pack_third,
        dict(far0=far0, far1=far1, gate=a.c1),
        dict(far=windows, near_edge=edge, send=(fields + 1, tall + EDGE, width)),
    )
    prev1 = moved("prev1", par.send, (2, 0), (-2, 0))
    b = call(
        outer,
        dict(far=par.far, next=after, next_edge=after_edge),
        dict(c7=coefs, f7=first, f8=first),
        [local(coefs)],
    )
    c = call(
        inner_last,
        dict(far=par.far, near5=near5, near_edge=par.near_edge, gate=prev0, c7=b.c7, f7=b.f7, f8=b.f8),
        dict(c6=coefs, f6=first, rel=rel, rel_edge=rel_edge),
    )
    last = moved("last", c.rel, (1, 0), (-1, 0))
    d = call(
        inner,
        dict(
            own=own.near,
            far=par.far,
            near5=near5,
            near4=near4,
            near_edge=par.near_edge,
            f6=c.f6,
            f7=b.f7,
            c6=c.c6,
        ),
        dict(c4=coefs, c5=coefs, f4=first, f5=first, rel=(2,) + rel, rel_edge=(2,) + rel_edge),
    )
    back = moved("back", d.rel, (1, 0), (-1, 0))
    n = call(
        near_rest,
        dict(
            near=own.near,
            near4=near4,
            near_edge=par.near_edge,
            f1=a.f1, f2=a.f2, c2=a.c2,
            f4=d.f4, f5=d.f5, c4=d.c4, rel=d.rel,
            rel7=c.rel,
        ),
        dict(rel=(2,) + rel, rel_edge=(2,) + rel_edge, rel4=rel, rel4_edge=rel_edge, sums=sums),
        [local(coefs), local(first)],
    )
    back4 = moved("back4", n.rel4, (1, 0), (-1, 0))
    r = call(
        far_rest,
        dict(
            prev0=prev0,
            prev1=prev1,
            far=own.far,
            f1=a.f1, f2=a.f2, c1=a.c1,
            sums=n.sums,
            gate=last,
        ),
        dict(rel=(2,) + rel, rel_edge=(2,) + rel_edge, sums=(devices,) + sums),
        [local(coefs)] * 2 + [local(first)] * 2 + [local(sums)],
    )
    totals = lax.all_to_all(r.sums, ("gz", "gy"), 0, 0)
    e = call(
        products,
        dict(
            own=r.rel,
            own_edge=r.rel_edge,
            mid=n.rel,
            mid_edge=n.rel_edge,
            rel4=n.rel4,
            rel4_edge=n.rel4_edge,
            rel=d.rel, rel_edge=d.rel_edge,
            rel7=c.rel,
            rel7_edge=c.rel_edge,
        ),
        dict(gram=gram, far=gram, mid=gram, both=(2 * gram[0], width)),
        [local((len(PAIRS) * tall, width)), local((len(PAIRS), groups * BLOCK, width // BLOCK))],
    )
    both = moved("both", e.both, (1, 0), (-1, 0))
    same = moved("same", e.far, (2, 0), (-2, 0))
    crossed = moved("crossed", e.gram, (-1, 0), (1, 0))
    finish = functools.partial(finish_own, float(cells))
    finish.__name__ = "finish_own"
    result = [
        local((planes, fields, half, width)),
        local((len(PAIRS), 2 * groups, width)),
        pltpu.SemaphoreType.DMA((planes,)),
    ]
    mine = call(
        finish,
        dict(totals=totals, gram=e.gram, same=same, mid=e.mid, far=r.rel, near=n.rel),
        dict(prolong=tv.shape, mine=(len(PAIRS), groups, width // BLOCK), scales=sums),
        result,
        far=("prolong",),
    )
    whole = call(
        finish_other,
        dict(
            last=last,
            back=back,
            back4=back4,
            both=both,
            cross=crossed,
            scales=mine.scales,
            mine=mine.mine,
            own_part=mine.prolong,
        ),
        dict(prolong=tv.shape, factors=(len(PAIRS), planes // BLOCK, rows // BLOCK, width // BLOCK)),
        result,
        far=("prolong", "own_part"),
        alias=dict(own_part="prolong"),
    )
    return whole.prolong, whole.factors


def solution(mesh):
    return jax.shard_map(
        body,
        mesh=mesh,
        in_specs=(P(None, "gz", "gy", None), P("gz", "gy", None)),
        out_specs=(P(None, "gz", "gy", None), P(None, "gz", "gy", None)),
        check_vma=False,
    )
```

```python
import functools
import types
import jax
import jax.numpy as jnp
from jax import lax
from jax.experimental import pallas as pl
from jax.experimental.pallas import tpu as pltpu
from jax.sharding import PartitionSpec as P

RELAX_WEIGHT = 2.0 / 3.0
PAIRS = ((0, 0), (0, 1), (0, 2), (0, 3), (1, 1), (1, 2), (1, 3), (2, 2), (2, 3), (3, 3))
AT = {pair: k for k, pair in enumerate(PAIRS)}
BLOCK = 4
EDGE = 8
VMEM_LIMIT = 40 * 1024 * 1024
FIRST_LIMIT = 60 * 1024 * 1024

COST = {'inner': 10, 'pack_near': 8, 'early': 3, 'arrived': 1, 'near_rest': 3}


def call(body, ins, outs, scratch=(), far=(), limit=VMEM_LIMIT):
    names_in, names_out = list(ins), list(outs)

    def kernel(*refs):
        cut = len(names_in) + len(names_out)
        i = types.SimpleNamespace(**dict(zip(names_in, refs)))
        o = types.SimpleNamespace(**dict(zip(names_out, refs[len(names_in) :])))
        body(i, o, *refs[cut:])

    def spec(name):
        return pl.BlockSpec(memory_space=pl.ANY if name in far or name == "gate" else pltpu.VMEM)

    got = pl.pallas_call(
        kernel,
        out_shape=[jax.ShapeDtypeStruct(outs[k], jnp.float32) for k in names_out],
        in_specs=[spec(k) for k in names_in],
        out_specs=[spec(k) for k in names_out],
        scratch_shapes=list(scratch),
        compiler_params=pltpu.CompilerParams(vmem_limit_bytes=limit),
        cost_estimate=pl.CostEstimate(flops=int(COST.get(body.__name__, 0) * 1e9), bytes_accessed=0, transcendentals=0),
        name=body.__name__,
    )(*[ins[k] for k in names_in])
    return types.SimpleNamespace(**dict(zip(names_out, got)))


def parity():
    return lax.rem(lax.axis_index("gz"), 2)


def natural(k, odd, planes):
    return k + odd * (planes - 1 - 2 * k)


def half_of_tile(shape):
    return lax.broadcasted_iota(jnp.int32, shape, 0) // BLOCK


def rows_at(start, size):
    return pl.ds(pl.multiple_of(start, 8), size)


def copies(jobs, sems):
    started = [pltpu.make_async_copy(a, b, sems.at[n]) for n, (a, b) in enumerate(jobs)]
    for one in started:
        one.start()
    return started


def plane_jobs(i, k, odd, start, target):
    fields, planes = i.tv.shape[:2]
    half = i.tv.shape[2] // 2
    at, rows = natural(k, odd, planes), rows_at(start, half)
    return [
        (i.tv.at[:, at, rows, :], target.at[pl.ds(0, fields), pl.ds(0, half), :]),
        (i.coef.at[at, rows, :], target.at[fields, pl.ds(0, half), :]),
    ]


def tile_jobs(i, start, target):
    fields, rows = i.tv.shape[0], rows_at(start, EDGE)
    return [
        (i.tv.at[:, :, rows, :], target.at[pl.ds(0, fields)]),
        (i.coef.at[:, rows, :], target.at[fields]),
    ]


def packed(tiles, q, f, side, odd, which):
    planes = tiles.shape[1]
    u, v = tiles[f, natural(2 * q, odd, planes)], tiles[f, natural(2 * q + 1, odd, planes)]
    return jnp.where(which == side, u, pltpu.roll(v, BLOCK, 0))


def unpacked(tile, k):
    return tile if k % 2 == 0 else pltpu.roll(tile, BLOCK, 0)


def pack_first(i, o, extra, halo, cross, edge, sems, late_sems):
    odd = parity()
    fields, planes, rows, width = i.tv.shape
    half = rows // 2
    jobs = tile_jobs(i, half - EDGE * (1 - odd), extra)
    jobs += tile_jobs(i, (rows - EDGE) * (1 - odd), halo) + tile_jobs(i, (rows - EDGE) * odd, cross)
    jobs += plane_jobs(i, 0, odd, (1 - odd) * half, o.far0)
    started = copies(jobs, sems)
    for one in started[:6]:
        one.wait()
    which = half_of_tile((EDGE, width))
    for q in range(planes // 2):
        for f in range(fields + 1):
            edge[q, f] = packed(extra, q, f, 1 - odd, odd, which)
            o.halo[q, f] = packed(halo, q, f, 1 - odd, odd, which)
            o.cross[q, f] = packed(cross, q, f, odd, odd, which)
    more = [(edge.at[q], o.far0.at[:, pl.ds(half + q * EDGE, EDGE), :]) for q in range(planes // 2)]
    o.mark[...] = jnp.zeros_like(o.mark)
    for one in started[6:] + copies(more, late_sems):
        one.wait()


def pack_own(i, o, sems):
    odd = parity()
    half = i.tv.shape[2] // 2
    jobs = []
    for k in range(2):
        jobs += plane_jobs(i, k, odd, odd * half, o.own.at[k])
    for one in copies(jobs, sems):
        one.wait()


def pack_second(i, o, extra, sems):
    odd = parity()
    fields, planes, rows, width = i.tv.shape
    half = rows // 2
    jobs = tile_jobs(i, half - EDGE * odd, extra)
    jobs += plane_jobs(i, 1, odd, (1 - odd) * half, o.far1)
    for k in range(2):
        jobs += plane_jobs(i, 2 + k, odd, odd * half, o.near.at[k])
    started = copies(jobs, sems)
    o.far[:, :, :half] = i.own[...]
    for q in range(planes // 2):
        o.far1[:, pl.ds(half + q * EDGE, EDGE), :] = i.cross[q]
    for one in started:
        one.wait()
    which = half_of_tile((EDGE, width))
    for k in range(planes):
        for f in range(fields + 1):
            own = extra[f, natural(k, odd, planes)]
            window_of = (o.far if k < 2 else o.near)
            tile = jnp.where(which == odd, own, unpacked(i.halo[k // 2, f], k))
            window_of[k % 2, f, half:] = tile
            if k < 2:
                o.far_edge[k, f] = tile


def pack_near(i, o, sems):
    odd = parity()
    half = i.tv.shape[2] // 2
    jobs = []
    for k in range(2):
        jobs += plane_jobs(i, 2 + k, odd, (1 - odd) * half, (o.send1 if k else o.send0))
    started = copies(jobs, sems)
    for one in started:
        one.wait()


def pack_third(i, o):
    odd = parity()
    fields, tall, width = i.far0.shape
    half = tall - 2 * EDGE
    which = half_of_tile((EDGE, width))
    for k in range(4):
        for f in range(fields):
            extra = i.far0[f, pl.ds(half + k // 2 * EDGE, EDGE), :]
            cross = i.far1[f, pl.ds(half + k // 2 * EDGE, EDGE), :]
            tile = jnp.where(which == odd, unpacked(extra, k), unpacked(cross, k))
            if k < 2:
                plane = (i.far1 if k else i.far0)[f, :half]
                o.far[k, f, :half] = plane
                o.far[k, f, half:] = tile
            else:
                o.near_edge[k - 2, f] = tile


def inverse(x):
    guess = pl.reciprocal(x, approx=True)
    return guess * (2.0 - x * guess)


def onward(x, axis):
    return pltpu.roll(x, x.shape[axis] - 1, axis)


def backward(x, axis):
    return pltpu.roll(x, 1, axis)


def joint(a, b):
    return a * b * inverse(a + b)


def weigh(before, here, after, c):
    wx = joint(here, onward(here, 1))
    wy = joint(here, onward(here, 0))
    wm = joint(here, before)
    wp = joint(here, after)
    c[0] = wx
    c[1] = wy
    c[2] = wm
    c[3] = wp
    c[4] = RELAX_WEIGHT * inverse(wx + backward(wx, 1) + wy + backward(wy, 0) + wm + wp)


def step(before, here, after, c):
    fx = c[0] * (here - onward(here, 1))
    fy = c[1] * (here - onward(here, 0))
    flux = (fx - backward(fx, 1)) + (fy - backward(fy, 0))
    flux = flux + c[2] * (here - before) + c[3] * (here - after)
    return here - c[4] * flux


def window(whole, at):
    return lambda f: whole[at, f]


def joined(keep, edge, at):
    return lambda f: jnp.concatenate([keep[f], edge[at, f]], axis=0)


def sweep_first(planes, z, c, out):
    last = 4
    weigh(planes[z - 1](last), planes[z](last), planes[z + 1](last), c)
    for f in range(last):
        out[f] = step(planes[z - 1](f), planes[z](f), planes[z + 1](f), c)


def sweep_second(first, z, c, keep, edge):
    half = keep.shape[1]
    for f in range(first[z].shape[0]):
        value = step(first[z - 1][f], first[z][f], first[z + 1][f], c)
        keep[f] = value[:half]
        edge[f] = value[half:]


def early(i, o):
    planes = {k: window(i.far, k) for k in (0, 1)} | {k + 2: window(i.near, k) for k in (0, 1)}
    sweep_first(planes, 1, o.c1, o.f1)
    sweep_first(planes, 2, o.c2, o.f2)


def outer(i, o, c8):
    planes = {7 - k: window(i.far, k) for k in (0, 1)}
    planes |= {8 + k: joined(i.next.at[k], i.next_edge, k) for k in (0, 1)}
    sweep_first(planes, 7, o.c7, o.f7)
    sweep_first(planes, 8, c8, o.f8)


def inner_last(i, o):
    planes = {7 - k: window(i.far, k) for k in (0, 1)} | {5: joined(i.near5, i.near_edge, 0)}
    sweep_first(planes, 6, o.c6, o.f6)
    sweep_second({6: o.f6, 7: i.f7, 8: i.f8}, 7, i.c7, o.rel, o.rel_edge)


def inner(i, o, c5, stacked, folded):
    planes = {3: window(i.own, 1), 6: window(i.far, 1)}
    planes |= {5 - k: joined((i.near4 if k else i.near5), i.near_edge, k) for k in (0, 1)}
    sweep_first(planes, 5, c5, o.f5)
    sweep_first(planes, 4, o.c4, o.f4)
    first = {4: o.f4, 5: o.f5, 6: i.f6, 7: i.f7}
    sweep_second(first, 6, i.c6, o.rel.at[0], o.rel_edge.at[0])
    sweep_second(first, 5, c5, o.rel.at[1], o.rel_edge.at[1])
    grams([(i.rel7, i.rel7_edge), (o.rel.at[0], o.rel_edge.at[0])], o.gram, stacked, folded)
    flat(o.send, [o.rel.at[0], o.rel.at[1]], o.gram)


def flat(send, planes, gram):
    fields, half = planes[0].shape[:2]
    for n, plane in enumerate(planes):
        for f in range(fields):
            send[pl.ds((n * fields + f) * half, half), :] = plane[f]
    send[pl.ds(len(planes) * fields * half, gram.shape[0]), :] = gram[...]


def squares(refs, sums, before=None):
    fields, half, width = refs[0].shape
    for f in range(fields):
        total = jnp.zeros((EDGE, width), jnp.float32)
        for ref in refs:
            for tile in range(half // EDGE):
                part = ref[f, pl.ds(tile * EDGE, EDGE), :]
                total = total + part * part
        total = jnp.sum(total[:, : width // 2] + total[:, width // 2 :], axis=0, keepdims=True)
        sums[f : f + 1] = total if before is None else total + before[f : f + 1]


def near_rest(i, o, c3, f3, stacked, folded):
    planes = {2: window(i.own, 0), 3: window(i.own, 1), 4: joined(i.near4, i.near_edge, 1)}
    sweep_first(planes, 3, c3, f3)
    first = {1: i.f1, 2: i.f2, 3: f3, 4: i.f4, 5: i.f5}
    sweep_second(first, 4, i.c4, o.rel.at[2], o.rel_edge.at[2])
    sweep_second(first, 2, i.c2, o.rel.at[0], o.rel_edge.at[0])
    sweep_second(first, 3, c3, o.rel.at[1], o.rel_edge.at[1])
    own = [(o.rel.at[k], o.rel_edge.at[k]) for k in range(3)]
    grams(own + [(i.rel.at[1], i.rel_edge.at[1])], o.gram, stacked, folded)
    flat(o.send, [o.rel.at[2]], o.gram)
    squares([o.rel.at[k] for k in range(3)] + [i.rel7, i.rel.at[0], i.rel.at[1]], o.sums)


def far_rest(i, o, cm, c0, fm, f0, own_sums):
    planes = {k: window(i.far, k) for k in (0, 1)} | {-1 - k: window(i.prev, k) for k in (0, 1)}
    sweep_first(planes, -1, cm, fm)
    sweep_first(planes, 0, c0, f0)
    first = {-1: fm, 0: f0, 1: i.f1, 2: i.f2}
    sweep_second(first, 0, c0, o.rel.at[0], o.rel_edge.at[0])
    sweep_second(first, 1, i.c1, o.rel.at[1], o.rel_edge.at[1])
    squares([o.rel.at[0], o.rel.at[1]], own_sums, i.sums)
    for n in range(o.sums.shape[0]):
        o.sums[n] = own_sums[...]


def split(x):
    high = x.astype(jnp.bfloat16)
    return high, (x - high.astype(jnp.float32)).astype(jnp.bfloat16)


def times_table(x, table):
    high, low = split(x)
    return jnp.dot(high, table, preferred_element_type=jnp.float32) + jnp.dot(
        low, table, preferred_element_type=jnp.float32
    )


def lane_table(width, spread):
    part = width // BLOCK
    shape = (part, width) if spread else (width, part)
    cell = lax.broadcasted_iota(jnp.int32, shape, 1 if spread else 0)
    block = lax.broadcasted_iota(jnp.int32, shape, 0 if spread else 1)
    moved = jnp.where(cell < 2, cell + width - 2, cell - 2)
    return (moved // BLOCK == block).astype(jnp.bfloat16)


def group_count(half):
    return (half // BLOCK + 1 + 7) // 8 * 8


def places(at, groups, part):
    row = at // BLOCK * groups
    if at < len(PAIRS) // BLOCK * BLOCK:
        return [(row, at % BLOCK * part, 0, groups)]
    low = groups // 2
    return [(row, (at % BLOCK + 2 * n) * part, n * low, low) for n in range(2)]


def grams(planes, out, stacked, folded):
    half, width = planes[0][0].shape[1:]
    tall, part, groups = half + EDGE, width // BLOCK, group_count(half)
    for at, (a, b) in enumerate(PAIRS):
        total = None
        for keep, edge in planes:
            left = jnp.concatenate([keep[a], edge[a]], axis=0)
            right = left if a == b else jnp.concatenate([keep[b], edge[b]], axis=0)
            total = left * right if total is None else total + left * right
        stacked[pl.ds(at * tall, tall), :] = total
    across = times_table(stacked[...], lane_table(width, False))
    for at in range(len(PAIRS)):
        two = across[at * tall : (at + 1) * tall]
        two = two + backward(two, 0)
        folded[at, :tall] = two + pltpu.roll(two, 2, 0)
        folded[at, tall:] = jnp.zeros((groups * BLOCK - tall, part), jnp.float32)
    for at in range(len(PAIRS)):
        value = folded[at, pl.ds(1, groups, stride=BLOCK), :]
        for row, lane, piece, size in places(at, groups, part):
            out[pl.ds(row, size), pl.ds(lane, part)] = value[piece : piece + size]


def far_products(i, o, stacked, folded):
    grams([(i.rel.at[k], i.rel_edge.at[k]) for k in range(2)], o.gram, stacked, folded)
    count = o.gram.shape[0]
    o.send[:count] = o.gram[...]
    o.send[count:] = i.back[pl.ds(i.back.shape[0] - count, count), :]


def arrived(i, o):
    o.mark[...] = jnp.zeros_like(o.mark)


def solve_rows(rels, spread, base, scale, result, z):
    fields, half, width = result.shape[1:]
    within = lax.broadcasted_iota(jnp.int32, (EDGE, width), 0)
    for tile in range(half // EDGE):
        entry = {}
        for at, key in enumerate(PAIRS):
            three = [jnp.broadcast_to(spread[at, pl.ds(base + 2 * tile + n, 1), :], (EDGE, width)) for n in range(3)]
            entry[key] = jnp.where(within < 2, three[0], jnp.where(within < 6, three[1], three[2]))
        rows = pl.ds(tile * EDGE, EDGE)
        for n, rel in enumerate(rels):
            columns = []
            for b in range(fields):
                accum = rel(b, tile) * scale[b]
                for a in range(b):
                    accum = accum - entry[a, b] * columns[a]
                columns.append(accum * entry[b, b])
                result[z + n, b, rows, :] = columns[b]


def write_plane(result, slot, z, prolong, start, odd, sems):
    planes, half = prolong.shape[1], result.shape[2]
    target = prolong.at[:, natural(z, odd, planes), rows_at(start, half), :]
    one = pltpu.make_async_copy(result.at[slot], target, sems.at[slot])
    one.start()
    return one


def triangle(scale, values):
    fields = len(scale)
    matrix = {(a, b): values(at) * (scale[a] * scale[b]) for at, (a, b) in enumerate(PAIRS)}
    trace = matrix[0, 0] + matrix[1, 1] + matrix[2, 2] + matrix[3, 3]
    ridge = 0.64 * (trace / 256.0 + 1e-06)
    upper, inv = {}, {}
    for a in range(fields):
        for b in range(a, fields):
            accum = matrix[a, b] + ridge if a == b else matrix[a, b]
            for c in range(a):
                accum = accum - upper[c, a] * upper[c, b]
            if a == b:
                upper[a, a] = jnp.sqrt(accum)
                inv[a] = 1.0 / upper[a, a]
            else:
                upper[a, b] = accum * inv[a]
    return upper, inv


def spread_all(upper, inv, lanes, spread):
    entries = [inv[a] if a == b else upper[a, b] for a, b in PAIRS]
    rows = entries[0].shape[0]
    wide = times_table(jnp.concatenate(entries, axis=0), lanes)
    for at in range(len(PAIRS)):
        spread[at] = wide[at * rows : (at + 1) * rows]


def gram_at(ref, at, groups, start=0):
    part = ref.shape[-1] // BLOCK
    pieces = [ref[pl.ds(start + row, size), pl.ds(lane, part)] for row, lane, _, size in places(at, groups, part)]
    return jnp.concatenate(pieces, axis=0)


def in_plane(ref):
    return lambda b, tile: ref[b, pl.ds(tile * EDGE, EDGE), :]


def in_flat(ref, n, fields, half):
    return lambda b, tile: ref[pl.ds((n * fields + b) * half + tile * EDGE, EDGE), :]


def finish_all(cells, i, o, result, spread, sems):
    odd = parity()
    fields, planes, rows, width = o.prolong.shape
    half = rows // 2
    groups = group_count(half)
    totals = jnp.sum(jnp.sum(i.totals[...], axis=0), axis=1, keepdims=True)
    scales = lax.rsqrt(totals / cells + 1e-06)
    scale = [scales[f : f + 1] for f in range(fields)]
    count = i.mid.shape[0]
    in_back, in_tail = i.back.shape[0] - count, i.tail.shape[0] - count

    def values(at):
        own_far = gram_at(i.gram, at, groups) + gram_at(i.cross, at, groups, count)
        other_far = gram_at(i.back, at, groups, in_back) + gram_at(i.cross, at, groups)
        return jnp.concatenate(
            [own_far, other_far, gram_at(i.mid, at, groups), gram_at(i.tail, at, groups, in_tail)], axis=0
        )

    upper, inv = triangle(scale, values)
    spread_all(upper, inv, lane_table(width, True), spread)
    writes = []
    for block, rels in enumerate(
        (
            [in_plane(i.far.at[k]) for k in range(2)],
            [in_plane(i.last), in_flat(i.back, 0, fields, half)],
            [in_plane(i.near.at[k]) for k in range(2)],
            [in_flat(i.back, 1, fields, half), in_flat(i.tail, 0, fields, half)],
        )
    ):
        z, side = block // 2 * 2, block % 2
        solve_rows(rels, spread, block * groups, scale, result, 2 * block)
        start = (side + odd - 2 * side * odd) * half
        writes += [write_plane(result, 2 * block + k, z + k, o.prolong, start, odd, sems) for k in range(2)]
    per_half = half // BLOCK
    line = lax.broadcasted_iota(jnp.int32, (2 * per_half, width // BLOCK), 0)
    pad = jnp.zeros((2 * per_half - groups, width // BLOCK), jnp.float32)
    for at, pair in enumerate(PAIRS):
        value = jnp.where(odd == 0, upper[pair][2 * groups :], upper[pair][: 2 * groups])
        mine, others = value[:groups], value[groups:]
        low = jnp.concatenate([jnp.where(odd == 0, mine, others), pad], axis=0)
        top = jnp.concatenate([jnp.where(odd == 0, others, mine), pad], axis=0)
        o.factors[at, 0] = jnp.where(line < per_half, onward(low, 0), pltpu.roll(top, per_half - 1, 0))
    for one in writes:
        one.wait()


def moved(x, even_by, odd_by):
    nz, ny = lax.axis_size("gz"), lax.axis_size("gy")
    route = []
    for z in range(nz):
        dz, dy = odd_by if z % 2 else even_by
        for y in range(ny):
            route.append((z * ny + y, (z + dz) % nz * ny + (y + dy) % ny))
    return lax.ppermute(x, ("gz", "gy"), route)


def body(tv, coef):
    fields, planes, rows, width = tv.shape
    half = rows // 2
    devices = lax.axis_size("gz") * lax.axis_size("gy")
    cells = devices * planes * rows * width
    groups = group_count(half)
    tall = half + EDGE
    windows, edge = (2, fields + 1, tall, width), (2, fields + 1, EDGE, width)
    keep, keeps = (fields + 1, half, width), (2, fields + 1, half, width)
    first, coefs = (fields, tall, width), (5, tall, width)
    gram = (len(PAIRS) // BLOCK * groups + groups // 2, width)
    sums = (8, width // 2)
    rel, rel_edge = (fields, half, width), (fields, EDGE, width)

    def local(shape):
        return pltpu.VMEM(shape, jnp.float32)

    tiles = local((fields + 1, planes, EDGE, width))
    args = dict(tv=tv, coef=coef)
    sent = call(
        pack_first,
        args,
        dict(far0=(fields + 1, half + 2 * EDGE, width), halo=edge, cross=edge, mark=sums),
        [tiles] * 3 + [local(edge), pltpu.SemaphoreType.DMA((8,)), pltpu.SemaphoreType.DMA((2,))],
        far=("tv", "coef"),
        limit=FIRST_LIMIT,
    )
    far_own = call(
        pack_own,
        dict(gate=sent.mark, **args),
        dict(own=keeps),
        [pltpu.SemaphoreType.DMA((4,))],
        far=("tv", "coef"),
    ).own
    far0 = moved(sent.far0, (1, 0), (-1, 0))
    halo = moved(sent.halo, (0, 1), (0, -1))
    cross = moved(sent.cross, (0, -1), (0, 1))
    after = moved(far_own, (-2, 0), (2, 0))
    own = call(
        pack_second,
        dict(halo=halo, cross=cross, own=far_own, **args),
        dict(
            far=windows,
            near=windows,
            far1=(fields + 1, half + 2 * EDGE, width),
            far_edge=edge,
        ),
        [tiles, pltpu.SemaphoreType.DMA((8,))],
        far=("tv", "coef"),
    )
    to_near = call(
        pack_near,
        dict(gate=far0, **args),
        dict(send0=keep, send1=keep),
        [pltpu.SemaphoreType.DMA((4,))],
        far=("tv", "coef"),
    )
    far1 = moved(own.far1, (1, 0), (-1, 0))
    near5 = moved(to_near.send0, (1, 0), (-1, 0))
    near4 = moved(to_near.send1, (1, 0), (-1, 0))
    after_edge = moved(own.far_edge, (-2, 0), (2, 0))
    a = call(
        early,
        dict(far=own.far, near=own.near),
        dict(c1=coefs, c2=coefs, f1=first, f2=first),
    )
    par = call(
        pack_third,
        dict(far0=far0, far1=far1),
        dict(far=windows, near_edge=edge),
    )
    before = moved(par.far, (2, 0), (-2, 0))
    b = call(
        outer,
        dict(far=par.far, next=after, next_edge=after_edge, gate=a.c1),
        dict(c7=coefs, f7=first, f8=first),
        [local(coefs)],
    )
    c = call(
        inner_last,
        dict(far=par.far, near5=near5, near_edge=par.near_edge, c7=b.c7, f7=b.f7, f8=b.f8),
        dict(c6=coefs, f6=first, rel=rel, rel_edge=rel_edge),
    )
    last = moved(c.rel, (1, 0), (-1, 0))
    sum_scratch = [local((len(PAIRS) * tall, width)), local((len(PAIRS), groups * BLOCK, width // BLOCK))]
    d = call(
        inner,
        dict(
            own=own.near,
            far=par.far,
            near5=near5,
            near4=near4,
            near_edge=par.near_edge,
            f6=c.f6,
            f7=b.f7,
            c6=c.c6,
            rel7=c.rel,
            rel7_edge=c.rel_edge,
        ),
        dict(
            c4=coefs,
            f4=first,
            f5=first,
            rel=(2,) + rel,
            rel_edge=(2,) + rel_edge,
            gram=gram,
            send=(2 * fields * half + gram[0], width),
        ),
        [local(coefs)] + sum_scratch,
    )
    back = moved(d.send, (1, 0), (-1, 0))
    n = call(
        near_rest,
        dict(
            own=own.near,
            near4=near4,
            near_edge=par.near_edge,
            f1=a.f1,
            f2=a.f2,
            f4=d.f4,
            f5=d.f5,
            c2=a.c2,
            c4=d.c4,
            rel=d.rel,
            rel_edge=d.rel_edge,
            rel7=c.rel,
        ),
        dict(
            rel=(3,) + rel,
            rel_edge=(3,) + rel_edge,
            gram=gram,
            send=(fields * half + gram[0], width),
            sums=sums,
        ),
        [local(coefs), local(first)] + sum_scratch,
    )
    tail = moved(n.send, (1, 0), (-1, 0))
    r = call(
        far_rest,
        dict(
            prev=before,
            far=own.far,
            f1=a.f1, f2=a.f2, c1=a.c1,
            sums=n.sums,
            gate=last,
        ),
        dict(rel=(2,) + rel, rel_edge=(2,) + rel_edge, sums=(devices,) + sums),
        [local(coefs)] * 2 + [local(first)] * 2 + [local(sums)],
    )
    totals = lax.all_to_all(r.sums, ("gz", "gy"), 0, 0)
    e = call(
        far_products,
        dict(rel=r.rel, rel_edge=r.rel_edge, back=back),
        dict(gram=gram, send=(2 * gram[0], width)),
        sum_scratch,
    )
    crossed = moved(e.send, (-1, 0), (1, 0))
    marked = call(arrived, dict(gate=tail, gram=e.gram), dict(mark=sums))
    finish = functools.partial(finish_all, float(cells))
    finish.__name__ = "finish_all"
    whole = call(
        finish,
        dict(
            totals=totals,
            gram=e.gram,
            cross=crossed,
            mid=n.gram,
            back=back,
            tail=tail,
            last=last,
            far=r.rel,
            near=n.rel,
            mark=marked.mark,
        ),
        dict(prolong=tv.shape, factors=(len(PAIRS), planes // BLOCK, rows // BLOCK, width // BLOCK)),
        [
            local((2 * planes, fields, half, width)),
            local((len(PAIRS), 4 * groups, width)),
            pltpu.SemaphoreType.DMA((2 * planes,)),
        ],
        far=("prolong",),
    )
    return whole.prolong, whole.factors


def solution(mesh):
    return jax.shard_map(
        body,
        mesh=mesh,
        in_specs=(P(None, "gz", "gy", None), P("gz", "gy", None)),
        out_specs=(P(None, "gz", "gy", None), P(None, "gz", "gy", None)),
        check_vma=False,
    )
```

```python
import functools
import types
import jax
import jax.numpy as jnp
from jax import lax
from jax.experimental import pallas as pl
from jax.experimental.pallas import tpu as pltpu
from jax.sharding import PartitionSpec as P

RELAX_WEIGHT = 2.0 / 3.0
PAIRS = ((0, 0), (0, 1), (0, 2), (0, 3), (1, 1), (1, 2), (1, 3), (2, 2), (2, 3), (3, 3))
AT = {pair: k for k, pair in enumerate(PAIRS)}
BLOCK = 4
EDGE = 8
VMEM_LIMIT = 40 * 1024 * 1024
FIRST_LIMIT = 60 * 1024 * 1024

COST = {'inner': 10, 'pack_near': 8, 'early': 3, 'arrived': 1, 'near_rest': 3}


def call(body, ins, outs, scratch=(), far=(), limit=VMEM_LIMIT):
    names_in, names_out = list(ins), list(outs)

    def kernel(*refs):
        cut = len(names_in) + len(names_out)
        i = types.SimpleNamespace(**dict(zip(names_in, refs)))
        o = types.SimpleNamespace(**dict(zip(names_out, refs[len(names_in) :])))
        body(i, o, *refs[cut:])

    def spec(name):
        return pl.BlockSpec(memory_space=pl.ANY if name in far or name == "gate" else pltpu.VMEM)

    got = pl.pallas_call(
        kernel,
        out_shape=[jax.ShapeDtypeStruct(outs[k], jnp.float32) for k in names_out],
        in_specs=[spec(k) for k in names_in],
        out_specs=[spec(k) for k in names_out],
        scratch_shapes=list(scratch),
        compiler_params=pltpu.CompilerParams(vmem_limit_bytes=limit),
        cost_estimate=pl.CostEstimate(flops=int(COST.get(body.__name__, 0) * 1e9), bytes_accessed=0, transcendentals=0),
        name=body.__name__,
    )(*[ins[k] for k in names_in])
    return types.SimpleNamespace(**dict(zip(names_out, got)))


def parity():
    return lax.rem(lax.axis_index("gz"), 2)


def natural(k, odd, planes):
    return k + odd * (planes - 1 - 2 * k)


def half_of_tile(shape):
    return lax.broadcasted_iota(jnp.int32, shape, 0) // BLOCK


def rows_at(start, size):
    return pl.ds(pl.multiple_of(start, 8), size)


def copies(jobs, sems):
    started = [pltpu.make_async_copy(a, b, sems.at[n]) for n, (a, b) in enumerate(jobs)]
    for one in started:
        one.start()
    return started


def plane_jobs(i, k, odd, start, target):
    fields, planes = i.tv.shape[:2]
    half = i.tv.shape[2] // 2
    at, rows = natural(k, odd, planes), rows_at(start, half)
    return [
        (i.tv.at[:, at, rows, :], target.at[pl.ds(0, fields), pl.ds(0, half), :]),
        (i.coef.at[at, rows, :], target.at[fields, pl.ds(0, half), :]),
    ]


def tile_jobs(i, start, target):
    fields, rows = i.tv.shape[0], rows_at(start, EDGE)
    return [
        (i.tv.at[:, :, rows, :], target.at[pl.ds(0, fields)]),
        (i.coef.at[:, rows, :], target.at[fields]),
    ]


def packed(tiles, q, f, side, odd, which):
    planes = tiles.shape[1]
    u, v = tiles[f, natural(2 * q, odd, planes)], tiles[f, natural(2 * q + 1, odd, planes)]
    return jnp.where(which == side, u, pltpu.roll(v, BLOCK, 0))


def unpacked(tile, k):
    return tile if k % 2 == 0 else pltpu.roll(tile, BLOCK, 0)


def pack_first(i, o, extra, halo, cross, edge, sems, late_sems):
    odd = parity()
    fields, planes, rows, width = i.tv.shape
    half = rows // 2
    jobs = tile_jobs(i, half - EDGE * (1 - odd), extra)
    jobs += tile_jobs(i, (rows - EDGE) * (1 - odd), halo) + tile_jobs(i, (rows - EDGE) * odd, cross)
    jobs += plane_jobs(i, 0, odd, (1 - odd) * half, o.far0)
    started = copies(jobs, sems)
    for one in started[:6]:
        one.wait()
    which = half_of_tile((EDGE, width))
    for q in range(planes // 2):
        for f in range(fields + 1):
            edge[q, f] = packed(extra, q, f, 1 - odd, odd, which)
            o.halo[q, f] = packed(halo, q, f, 1 - odd, odd, which)
            o.cross[q, f] = packed(cross, q, f, odd, odd, which)
    more = [(edge.at[q], o.far0.at[:, pl.ds(half + q * EDGE, EDGE), :]) for q in range(planes // 2)]
    for one in started[6:] + copies(more, late_sems):
        one.wait()


def pack_own(i, o, sems):
    odd = parity()
    half = i.tv.shape[2] // 2
    jobs = []
    for k in range(2):
        jobs += plane_jobs(i, k, odd, odd * half, o.own.at[k])
    for one in copies(jobs, sems):
        one.wait()


def pack_second(i, o, extra, sems):
    odd = parity()
    fields, planes, rows, width = i.tv.shape
    half = rows // 2
    jobs = tile_jobs(i, half - EDGE * odd, extra)
    jobs += plane_jobs(i, 1, odd, (1 - odd) * half, o.far1)
    for k in range(2):
        jobs += plane_jobs(i, 2 + k, odd, odd * half, o.near.at[k])
    started = copies(jobs, sems)
    o.far[:, :, :half] = i.own[...]
    for q in range(planes // 2):
        o.far1[:, pl.ds(half + q * EDGE, EDGE), :] = i.cross[q]
    for one in started:
        one.wait()
    which = half_of_tile((EDGE, width))
    for k in range(planes):
        for f in range(fields + 1):
            own = extra[f, natural(k, odd, planes)]
            window_of = (o.far if k < 2 else o.near)
            tile = jnp.where(which == odd, own, unpacked(i.halo[k // 2, f], k))
            window_of[k % 2, f, half:] = tile
            if k < 2:
                o.far_edge[k, f] = tile


def pack_near(i, o, sems):
    odd = parity()
    half = i.tv.shape[2] // 2
    jobs = []
    for k in range(2):
        jobs += plane_jobs(i, 2 + k, odd, (1 - odd) * half, (o.send1 if k else o.send0))
    started = copies(jobs, sems)
    for one in started:
        one.wait()


def pack_third(i, o):
    odd = parity()
    fields, tall, width = i.far0.shape
    half = tall - 2 * EDGE
    which = half_of_tile((EDGE, width))
    for k in range(4):
        for f in range(fields):
            extra = i.far0[f, pl.ds(half + k // 2 * EDGE, EDGE), :]
            cross = i.far1[f, pl.ds(half + k // 2 * EDGE, EDGE), :]
            tile = jnp.where(which == odd, unpacked(extra, k), unpacked(cross, k))
            if k < 2:
                plane = (i.far1 if k else i.far0)[f, :half]
                o.far[k, f, :half] = plane
                o.far[k, f, half:] = tile
            else:
                o.near_edge[k - 2, f] = tile


def inverse(x):
    guess = pl.reciprocal(x, approx=True)
    return guess * (2.0 - x * guess)


def onward(x, axis):
    return pltpu.roll(x, x.shape[axis] - 1, axis)


def backward(x, axis):
    return pltpu.roll(x, 1, axis)


def joint(a, b):
    return a * b * inverse(a + b)


def weigh(before, here, after, c):
    wx = joint(here, onward(here, 1))
    wy = joint(here, onward(here, 0))
    wm = joint(here, before)
    wp = joint(here, after)
    c[0] = wx
    c[1] = wy
    c[2] = wm
    c[3] = wp
    c[4] = RELAX_WEIGHT * inverse(wx + backward(wx, 1) + wy + backward(wy, 0) + wm + wp)


def step(before, here, after, c):
    fx = c[0] * (here - onward(here, 1))
    fy = c[1] * (here - onward(here, 0))
    flux = (fx - backward(fx, 1)) + (fy - backward(fy, 0))
    flux = flux + c[2] * (here - before) + c[3] * (here - after)
    return here - c[4] * flux


def window(whole, at):
    return lambda f: whole[at, f]


def joined(keep, edge, at):
    return lambda f: jnp.concatenate([keep[f], edge[at, f]], axis=0)


def sweep_first(planes, z, c, out):
    last = 4
    weigh(planes[z - 1](last), planes[z](last), planes[z + 1](last), c)
    for f in range(last):
        out[f] = step(planes[z - 1](f), planes[z](f), planes[z + 1](f), c)


def sweep_second(first, z, c, keep, edge):
    half = keep.shape[1]
    for f in range(first[z].shape[0]):
        value = step(first[z - 1][f], first[z][f], first[z + 1][f], c)
        keep[f] = value[:half]
        edge[f] = value[half:]


def early(i, o):
    planes = {k: window(i.far, k) for k in (0, 1)} | {k + 2: window(i.near, k) for k in (0, 1)}
    sweep_first(planes, 1, o.c1, o.f1)
    sweep_first(planes, 2, o.c2, o.f2)


def outer(i, o, c8):
    planes = {7 - k: window(i.far, k) for k in (0, 1)}
    planes |= {8 + k: joined(i.next.at[k], i.next_edge, k) for k in (0, 1)}
    sweep_first(planes, 7, o.c7, o.f7)
    sweep_first(planes, 8, c8, o.f8)


def inner_last(i, o):
    planes = {7 - k: window(i.far, k) for k in (0, 1)} | {5: joined(i.near5, i.near_edge, 0)}
    sweep_first(planes, 6, o.c6, o.f6)
    sweep_second({6: o.f6, 7: i.f7, 8: i.f8}, 7, i.c7, o.rel, o.rel_edge)


def inner(i, o, c5, stacked, folded):
    planes = {3: window(i.own, 1), 6: window(i.far, 1)}
    planes |= {5 - k: joined((i.near4 if k else i.near5), i.near_edge, k) for k in (0, 1)}
    sweep_first(planes, 5, c5, o.f5)
    sweep_first(planes, 4, o.c4, o.f4)
    first = {4: o.f4, 5: o.f5, 6: i.f6, 7: i.f7}
    sweep_second(first, 6, i.c6, o.rel.at[0], o.rel_edge.at[0])
    sweep_second(first, 5, c5, o.rel.at[1], o.rel_edge.at[1])
    grams([(i.rel7, i.rel7_edge), (o.rel.at[0], o.rel_edge.at[0])], o.gram, stacked, folded)
    flat(o.send, [o.rel.at[0], o.rel.at[1]], o.gram)


def flat(send, planes, gram):
    fields, half = planes[0].shape[:2]
    for n, plane in enumerate(planes):
        for f in range(fields):
            send[pl.ds((n * fields + f) * half, half), :] = plane[f]
    send[pl.ds(len(planes) * fields * half, gram.shape[0]), :] = gram[...]


def squares(refs, sums, before=None):
    fields, half, width = refs[0].shape
    for f in range(fields):
        total = jnp.zeros((EDGE, width), jnp.float32)
        for ref in refs:
            for tile in range(half // EDGE):
                part = ref[f, pl.ds(tile * EDGE, EDGE), :]
                total = total + part * part
        total = jnp.sum(total[:, : width // 2] + total[:, width // 2 :], axis=0, keepdims=True)
        sums[f : f + 1] = total if before is None else total + before[f : f + 1]


def near_rest(i, o, c3, f3, stacked, folded):
    planes = {2: window(i.own, 0), 3: window(i.own, 1), 4: joined(i.near4, i.near_edge, 1)}
    sweep_first(planes, 3, c3, f3)
    first = {1: i.f1, 2: i.f2, 3: f3, 4: i.f4, 5: i.f5}
    sweep_second(first, 4, i.c4, o.rel.at[2], o.rel_edge.at[2])
    sweep_second(first, 2, i.c2, o.rel.at[0], o.rel_edge.at[0])
    sweep_second(first, 3, c3, o.rel.at[1], o.rel_edge.at[1])
    own = [(o.rel.at[k], o.rel_edge.at[k]) for k in range(3)]
    grams(own + [(i.rel.at[1], i.rel_edge.at[1])], o.gram, stacked, folded)
    flat(o.send, [o.rel.at[2]], o.gram)
    squares([o.rel.at[k] for k in range(3)] + [i.rel7, i.rel.at[0], i.rel.at[1]], o.sums)


def far_rest(i, o, cm, c0, fm, f0, own_sums):
    planes = {k: window(i.far, k) for k in (0, 1)} | {-1 - k: window(i.prev, k) for k in (0, 1)}
    sweep_first(planes, -1, cm, fm)
    sweep_first(planes, 0, c0, f0)
    first = {-1: fm, 0: f0, 1: i.f1, 2: i.f2}
    sweep_second(first, 0, c0, o.rel.at[0], o.rel_edge.at[0])
    sweep_second(first, 1, i.c1, o.rel.at[1], o.rel_edge.at[1])
    squares([o.rel.at[0], o.rel.at[1]], own_sums, i.sums)
    for n in range(o.sums.shape[0]):
        o.sums[n] = own_sums[...]


def split(x):
    high = x.astype(jnp.bfloat16)
    return high, (x - high.astype(jnp.float32)).astype(jnp.bfloat16)


def times_table(x, table):
    high, low = split(x)
    return jnp.dot(high, table, preferred_element_type=jnp.float32) + jnp.dot(
        low, table, preferred_element_type=jnp.float32
    )


def lane_table(width, spread):
    part = width // BLOCK
    shape = (part, width) if spread else (width, part)
    cell = lax.broadcasted_iota(jnp.int32, shape, 1 if spread else 0)
    block = lax.broadcasted_iota(jnp.int32, shape, 0 if spread else 1)
    moved = jnp.where(cell < 2, cell + width - 2, cell - 2)
    return (moved // BLOCK == block).astype(jnp.bfloat16)


def group_count(half):
    return (half // BLOCK + 1 + 7) // 8 * 8


def places(at, groups, part):
    row = at // BLOCK * groups
    if at < len(PAIRS) // BLOCK * BLOCK:
        return [(row, at % BLOCK * part, 0, groups)]
    low = groups // 2
    return [(row, (at % BLOCK + 2 * n) * part, n * low, low) for n in range(2)]


def grams(planes, out, stacked, folded):
    half, width = planes[0][0].shape[1:]
    tall, part, groups = half + EDGE, width // BLOCK, group_count(half)
    for at, (a, b) in enumerate(PAIRS):
        total = None
        for keep, edge in planes:
            left = jnp.concatenate([keep[a], edge[a]], axis=0)
            right = left if a == b else jnp.concatenate([keep[b], edge[b]], axis=0)
            total = left * right if total is None else total + left * right
        stacked[pl.ds(at * tall, tall), :] = total
    across = times_table(stacked[...], lane_table(width, False))
    for at in range(len(PAIRS)):
        two = across[at * tall : (at + 1) * tall]
        two = two + backward(two, 0)
        folded[at, :tall] = two + pltpu.roll(two, 2, 0)
        folded[at, tall:] = jnp.zeros((groups * BLOCK - tall, part), jnp.float32)
    for at in range(len(PAIRS)):
        value = folded[at, pl.ds(1, groups, stride=BLOCK), :]
        for row, lane, piece, size in places(at, groups, part):
            out[pl.ds(row, size), pl.ds(lane, part)] = value[piece : piece + size]


def far_products(i, o, stacked, folded):
    grams([(i.rel.at[k], i.rel_edge.at[k]) for k in range(2)], o.gram, stacked, folded)


def both_sums(i, o):
    count = i.gram.shape[0]
    o.send[:count] = i.gram[...]
    o.send[count:] = i.back[pl.ds(i.back.shape[0] - count, count), :]


def arrived(i, o):
    o.mark[...] = jnp.zeros_like(o.mark)


def solve_rows(rels, spread, base, scale, result, z):
    fields, half, width = result.shape[1:]
    within = lax.broadcasted_iota(jnp.int32, (EDGE, width), 0)
    for tile in range(half // EDGE):
        entry = {}
        for at, key in enumerate(PAIRS):
            three = [jnp.broadcast_to(spread[at, pl.ds(base + 2 * tile + n, 1), :], (EDGE, width)) for n in range(3)]
            entry[key] = jnp.where(within < 2, three[0], jnp.where(within < 6, three[1], three[2]))
        rows = pl.ds(tile * EDGE, EDGE)
        for n, rel in enumerate(rels):
            columns = []
            for b in range(fields):
                accum = rel(b, tile) * scale[b]
                for a in range(b):
                    accum = accum - entry[a, b] * columns[a]
                columns.append(accum * entry[b, b])
                result[z + n, b, rows, :] = columns[b]


def write_plane(result, slot, z, prolong, start, odd, sems):
    planes, half = prolong.shape[1], result.shape[2]
    target = prolong.at[:, natural(z, odd, planes), rows_at(start, half), :]
    one = pltpu.make_async_copy(result.at[slot], target, sems.at[slot])
    one.start()
    return one


def triangle(scale, values):
    fields = len(scale)
    matrix = {(a, b): values(at) * (scale[a] * scale[b]) for at, (a, b) in enumerate(PAIRS)}
    trace = matrix[0, 0] + matrix[1, 1] + matrix[2, 2] + matrix[3, 3]
    ridge = 0.64 * (trace / 256.0 + 1e-06)
    upper, inv = {}, {}
    for a in range(fields):
        for b in range(a, fields):
            accum = matrix[a, b] + ridge if a == b else matrix[a, b]
            for c in range(a):
                accum = accum - upper[c, a] * upper[c, b]
            if a == b:
                upper[a, a] = jnp.sqrt(accum)
                inv[a] = 1.0 / upper[a, a]
            else:
                upper[a, b] = accum * inv[a]
    return upper, inv


def spread_all(upper, inv, lanes, spread):
    entries = [inv[a] if a == b else upper[a, b] for a, b in PAIRS]
    rows = entries[0].shape[0]
    wide = times_table(jnp.concatenate(entries, axis=0), lanes)
    for at in range(len(PAIRS)):
        spread[at] = wide[at * rows : (at + 1) * rows]


def gram_at(ref, at, groups, start=0):
    part = ref.shape[-1] // BLOCK
    pieces = [ref[pl.ds(start + row, size), pl.ds(lane, part)] for row, lane, _, size in places(at, groups, part)]
    return jnp.concatenate(pieces, axis=0)


def in_plane(ref):
    return lambda b, tile: ref[b, pl.ds(tile * EDGE, EDGE), :]


def in_flat(ref, n, fields, half):
    return lambda b, tile: ref[pl.ds((n * fields + b) * half + tile * EDGE, EDGE), :]


def finish_all(cells, i, o, result, spread, sems):
    odd = parity()
    fields, planes, rows, width = o.prolong.shape
    half = rows // 2
    groups = group_count(half)
    totals = jnp.sum(jnp.sum(i.totals[...], axis=0), axis=1, keepdims=True)
    scales = lax.rsqrt(totals / cells + 1e-06)
    scale = [scales[f : f + 1] for f in range(fields)]
    count = i.mid.shape[0]
    in_back, in_tail = i.back.shape[0] - count, i.tail.shape[0] - count

    def values(at):
        own_far = gram_at(i.gram, at, groups) + gram_at(i.cross, at, groups, count)
        other_far = gram_at(i.back, at, groups, in_back) + gram_at(i.cross, at, groups)
        return jnp.concatenate(
            [own_far, other_far, gram_at(i.mid, at, groups), gram_at(i.tail, at, groups, in_tail)], axis=0
        )

    upper, inv = triangle(scale, values)
    spread_all(upper, inv, lane_table(width, True), spread)
    writes = []
    for block, rels in enumerate(
        (
            [in_plane(i.far.at[k]) for k in range(2)],
            [in_plane(i.last), in_flat(i.back, 0, fields, half)],
            [in_plane(i.near.at[k]) for k in range(2)],
            [in_flat(i.back, 1, fields, half), in_flat(i.tail, 0, fields, half)],
        )
    ):
        z, side = block // 2 * 2, block % 2
        solve_rows(rels, spread, block * groups, scale, result, 2 * block)
        start = (side + odd - 2 * side * odd) * half
        writes += [write_plane(result, 2 * block + k, z + k, o.prolong, start, odd, sems) for k in range(2)]
    per_half = half // BLOCK
    line = lax.broadcasted_iota(jnp.int32, (2 * per_half, width // BLOCK), 0)
    pad = jnp.zeros((2 * per_half - groups, width // BLOCK), jnp.float32)
    for at, pair in enumerate(PAIRS):
        value = jnp.where(odd == 0, upper[pair][2 * groups :], upper[pair][: 2 * groups])
        mine, others = value[:groups], value[groups:]
        low = jnp.concatenate([jnp.where(odd == 0, mine, others), pad], axis=0)
        top = jnp.concatenate([jnp.where(odd == 0, others, mine), pad], axis=0)
        o.factors[at, 0] = jnp.where(line < per_half, onward(low, 0), pltpu.roll(top, per_half - 1, 0))
    for one in writes:
        one.wait()


def moved(x, even_by, odd_by):
    nz, ny = lax.axis_size("gz"), lax.axis_size("gy")
    route = []
    for z in range(nz):
        dz, dy = odd_by if z % 2 else even_by
        for y in range(ny):
            route.append((z * ny + y, (z + dz) % nz * ny + (y + dy) % ny))
    return lax.ppermute(x, ("gz", "gy"), route)


def body(tv, coef):
    fields, planes, rows, width = tv.shape
    half = rows // 2
    devices = lax.axis_size("gz") * lax.axis_size("gy")
    cells = devices * planes * rows * width
    groups = group_count(half)
    tall = half + EDGE
    windows, edge = (2, fields + 1, tall, width), (2, fields + 1, EDGE, width)
    keep, keeps = (fields + 1, half, width), (2, fields + 1, half, width)
    first, coefs = (fields, tall, width), (5, tall, width)
    gram = (len(PAIRS) // BLOCK * groups + groups // 2, width)
    sums = (8, width // 2)
    rel, rel_edge = (fields, half, width), (fields, EDGE, width)

    def local(shape):
        return pltpu.VMEM(shape, jnp.float32)

    tiles = local((fields + 1, planes, EDGE, width))
    args = dict(tv=tv, coef=coef)
    sent = call(
        pack_first,
        args,
        dict(far0=(fields + 1, half + 2 * EDGE, width), halo=edge, cross=edge),
        [tiles] * 3 + [local(edge), pltpu.SemaphoreType.DMA((8,)), pltpu.SemaphoreType.DMA((2,))],
        far=("tv", "coef"),
        limit=FIRST_LIMIT,
    )
    far_own = call(
        pack_own,
        args,
        dict(own=keeps),
        [pltpu.SemaphoreType.DMA((4,))],
        far=("tv", "coef"),
    ).own
    far0 = moved(sent.far0, (1, 0), (-1, 0))
    halo = moved(sent.halo, (0, 1), (0, -1))
    cross = moved(sent.cross, (0, -1), (0, 1))
    after = moved(far_own, (-2, 0), (2, 0))
    own = call(
        pack_second,
        dict(halo=halo, cross=cross, own=far_own, **args),
        dict(
            far=windows,
            near=windows,
            far1=(fields + 1, half + 2 * EDGE, width),
            far_edge=edge,
        ),
        [tiles, pltpu.SemaphoreType.DMA((8,))],
        far=("tv", "coef"),
    )
    to_near = call(
        pack_near,
        dict(gate=far0, **args),
        dict(send0=keep, send1=keep),
        [pltpu.SemaphoreType.DMA((4,))],
        far=("tv", "coef"),
    )
    far1 = moved(own.far1, (1, 0), (-1, 0))
    near5 = moved(to_near.send0, (1, 0), (-1, 0))
    near4 = moved(to_near.send1, (1, 0), (-1, 0))
    after_edge = moved(own.far_edge, (-2, 0), (2, 0))
    a = call(
        early,
        dict(far=own.far, near=own.near),
        dict(c1=coefs, c2=coefs, f1=first, f2=first),
    )
    par = call(
        pack_third,
        dict(far0=far0, far1=far1),
        dict(far=windows, near_edge=edge),
    )
    before = moved(par.far, (2, 0), (-2, 0))
    b = call(
        outer,
        dict(far=par.far, next=after, next_edge=after_edge, gate=a.c1),
        dict(c7=coefs, f7=first, f8=first),
        [local(coefs)],
    )
    c = call(
        inner_last,
        dict(far=par.far, near5=near5, near_edge=par.near_edge, c7=b.c7, f7=b.f7, f8=b.f8),
        dict(c6=coefs, f6=first, rel=rel, rel_edge=rel_edge),
    )
    last = moved(c.rel, (1, 0), (-1, 0))
    sum_scratch = [local((len(PAIRS) * tall, width)), local((len(PAIRS), groups * BLOCK, width // BLOCK))]
    d = call(
        inner,
        dict(
            own=own.near,
            far=par.far,
            near5=near5,
            near4=near4,
            near_edge=par.near_edge,
            f6=c.f6,
            f7=b.f7,
            c6=c.c6,
            rel7=c.rel,
            rel7_edge=c.rel_edge,
        ),
        dict(
            c4=coefs,
            f4=first,
            f5=first,
            rel=(2,) + rel,
            rel_edge=(2,) + rel_edge,
            gram=gram,
            send=(2 * fields * half + gram[0], width),
        ),
        [local(coefs)] + sum_scratch,
    )
    back = moved(d.send, (1, 0), (-1, 0))
    n = call(
        near_rest,
        dict(
            own=own.near,
            near4=near4,
            near_edge=par.near_edge,
            f1=a.f1,
            f2=a.f2,
            f4=d.f4,
            f5=d.f5,
            c2=a.c2,
            c4=d.c4,
            rel=d.rel,
            rel_edge=d.rel_edge,
            rel7=c.rel,
        ),
        dict(
            rel=(3,) + rel,
            rel_edge=(3,) + rel_edge,
            gram=gram,
            send=(fields * half + gram[0], width),
            sums=sums,
        ),
        [local(coefs), local(first)] + sum_scratch,
    )
    tail = moved(n.send, (1, 0), (-1, 0))
    r = call(
        far_rest,
        dict(
            prev=before,
            far=own.far,
            f1=a.f1, f2=a.f2, c1=a.c1,
            sums=n.sums,
            gate=last,
        ),
        dict(rel=(2,) + rel, rel_edge=(2,) + rel_edge, sums=(devices,) + sums),
        [local(coefs)] * 2 + [local(first)] * 2 + [local(sums)],
    )
    totals = lax.all_to_all(r.sums, ("gz", "gy"), 0, 0)
    e = call(
        far_products,
        dict(rel=r.rel, rel_edge=r.rel_edge),
        dict(gram=gram),
        sum_scratch,
    )
    pair = call(both_sums, dict(gram=e.gram, back=back), dict(send=(2 * gram[0], width)))
    crossed = moved(pair.send, (-1, 0), (1, 0))
    marked = call(arrived, dict(gate=tail, gram=pair.send), dict(mark=sums))
    finish = functools.partial(finish_all, float(cells))
    finish.__name__ = "finish_all"
    whole = call(
        finish,
        dict(
            totals=totals,
            gram=e.gram,
            cross=crossed,
            mid=n.gram,
            back=back,
            tail=tail,
            last=last,
            far=r.rel,
            near=n.rel,
            mark=marked.mark,
        ),
        dict(prolong=tv.shape, factors=(len(PAIRS), planes // BLOCK, rows // BLOCK, width // BLOCK)),
        [
            local((2 * planes, fields, half, width)),
            local((len(PAIRS), 4 * groups, width)),
            pltpu.SemaphoreType.DMA((2 * planes,)),
        ],
        far=("prolong",),
    )
    return whole.prolong, whole.factors


def solution(mesh):
    return jax.shard_map(
        body,
        mesh=mesh,
        in_specs=(P(None, "gz", "gy", None), P("gz", "gy", None)),
        out_specs=(P(None, "gz", "gy", None), P(None, "gz", "gy", None)),
        check_vma=False,
    )
```
